32 devices in a mesh: rev: 4 (over y, x), cust: 4 (over z), prod: 2 (over core).
Axes of the slice: x: 2, y: 2, z: 4, core: 2. Of those that a mesh axis runs over, the one named last changes fastest.
Arguments:
- review_cols: bfloat16 [16384, 2048], P(('rev', 'cust', 'prod')), may hold values from -24 to 24
- cust_state: bfloat16 [8192, 512], P(('rev', 'cust')), may hold values from -6 to 6
- prod_state: bfloat16 [4096, 512], P(('cust', 'prod')), may hold values from -6 to 6
- w_qkv: bfloat16 [512, 1536], replicated, may hold values from -0.25 to 0.25
- w_out: bfloat16 [512, 512], replicated, may hold values from -0.25 to 0.25
- w_msg: bfloat16 [512, 1024], replicated, may hold values from -0.25 to 0.25
- w_cust_up: bfloat16 [512, 512], replicated, may hold values from -0.25 to 0.25
- w_prod_up: bfloat16 [512, 512], replicated, may hold values from -0.25 to 0.25
- w_back: bfloat16 [1024, 512], replicated, may hold values from -0.1875 to 0.1875
- cust_slot: int32 [16384], P(('rev', 'cust', 'prod')), may hold values from 0 to 511
- prod_slot: int32 [16384], P(('rev', 'cust', 'prod')), may hold values from 0 to 511
- prod_pos: int32 [32, 512], P(('rev', 'cust', 'prod')), may hold values from 0 to 511, each once within a row
- live_count: int32 [32, 16], P(('rev', 'cust', 'prod')), may hold values from 1 to 32, 264 in all within a row
Outputs:
- review_out: bfloat16 [16384, 512], P(('rev', 'cust', 'prod'))
- new_cust: bfloat16 [8192, 512], P(('rev', 'cust'))
- new_prod: bfloat16 [4096, 512], P(('cust', 'prod'))
The draws below stay inside these ranges and needn't reach their ends.
Inputs may be any that keep to these rules, and one draw needn't show every extreme that they name: `prod_pos`: each device's row is a permutation of 0 to 511. `live_count`: each device's counts sum to 264, and some block holds 32 live reviews.
All inputs are finite; a program needn't handle non-finite values.
Results may differ from the reference program's by a relative error of at most 0.011.
Values may be sent and summed in bfloat16 or wider, within the bound.
No kernel may reach another device: no remote copies, remote signals or barrier semaphores. Data moves between devices by JAX's collectives and lax.ppermute only.
A program may use at most 128 MiB of HBM per device.

```python
import math
import jax
import jax.numpy as jnp
import numpy as np
from jax import lax

H = 512
HEADS = 8
NCOL = 4
R_DEV = 512
C_ROWS = 512
P_ROWS = 512
HD = 64
CSLOT = 32
PCAP = 64
LIVE = 264
REVIEWS = 16384
CUSTOMERS = 8192
PRODUCTS = 4096
N_REV = 4
N_CUST = 4
DEVICES = 32


def draw_review_cols(key, part):
    first_key = jax.random.fold_in(key, 0)
    result = jnp.clip(jax.random.normal(first_key, (REVIEWS, NCOL * H), jnp.float32), -6.0, 6.0)
    return result.astype(jnp.bfloat16)


def with_ends(values, own_key, smallest, largest):
    index_at = [jax.random.randint(jax.random.fold_in(own_key, axis), (), 0, length) for axis, length in enumerate(values.shape)]
    longest = values.shape.index(max(values.shape))
    beside = index_at[:longest] + [(index_at[longest] + 1) % values.shape[longest]] + index_at[longest + 1:]
    return values.at[tuple(index_at)].set(smallest).at[tuple(beside)].set(largest)


def block_scale(key, shape, shards, low, largest):
    loudness, own = 1.0, jax.random.fold_in(key, 6)
    for dim, shards_of in shards:
        steps = jnp.exp(jax.random.uniform(jax.random.fold_in(own, dim), (shards_of,), jnp.float32, low / len(shards), largest / len(shards)))
        loudness = loudness * jnp.repeat(steps, shape[dim] // shards_of).reshape([-1 if axis == dim else 1 for axis in range(len(shape))])
    return loudness


def rank_table(amount, lean):
    loads = [(1 << 20) // math.isqrt(rank ** lean) + 1 for rank in range(1, amount + 1)]
    spread = 1 + sum(loads) // (1 << 30)
    return np.cumsum(np.array([max(1, weight // spread) for weight in loads]))


def ranked(own_key, extent, amount, lean):
    listing = rank_table(amount, lean)
    pick = jax.random.randint(jax.random.fold_in(own_key, 1), extent, 0, int(listing[amount - 1]))
    grade = jnp.searchsorted(jnp.asarray(listing, jnp.int32), pick, side="right")
    return jax.random.permutation(jax.random.fold_in(own_key, 2), amount)[grade].astype(jnp.int32)


def length_profile(amount, total, limit, lean):
    weights = [(1 << 20) // math.isqrt(grade ** lean) + 1 for grade in range(2, amount + 1)]
    rest, given = total - limit - (amount - 1), [1] * (amount - 1)
    while rest > 0:
        free = [i for i in range(amount - 1) if given[i] < limit]
        mass, remaining = sum([weights[i] for i in free]), rest
        for i in free:
            addition = min(limit - given[i], max(1, remaining * weights[i] // mass), rest)
            given[i] = given[i] + addition
            rest = rest - addition
    return np.array([limit] + given)


def ragged_sizes(stream_key, number_of, total, bound, skew):
    if number_of == 2:
        one = jax.random.randint(stream_key, (), max(1, total - bound), min(bound, total - 1) + 1)
        return jnp.stack([one, total - one])
    tallies = jnp.asarray(length_profile(number_of, total, bound, skew), jnp.int32)
    pairs = (number_of - 1) // 2
    source_of, receiver = tallies[1:1 + 2 * pairs:2], tallies[2:2 + 2 * pairs:2]
    slack = jnp.minimum(source_of - 1, bound - receiver)
    shifted = jax.random.randint(jax.random.fold_in(stream_key, 1), (pairs,), 0, 1 << 20) % (slack + 1)
    tallies = tallies.at[1:1 + 2 * pairs:2].set(source_of - shifted).at[2:2 + 2 * pairs:2].set(receiver + shifted)
    return tallies[jax.random.permutation(jax.random.fold_in(stream_key, 2), number_of)]


def noise(own_key, extent, scale, most, pieces=(), kind=jnp.bfloat16):
    drawn = jax.random.normal(own_key, extent, jnp.float32) * scale
    if len(pieces) > 0:
        drawn = block_scale(own_key, extent, pieces, -0.22, 0.18) * drawn
    return jnp.clip(drawn, min=-most, max=most).astype(kind)


def setup_inputs(seed: int = 0) -> dict:
    keys = jax.random.split(jax.random.key(seed), 14)
    review_cols = draw_review_cols(jax.random.fold_in(keys[13], 71), 0)
    cust_state = noise(keys[1], (CUSTOMERS, H), 1.0, 6.0, ((0, 16),))
    prod_state = noise(keys[2], (PRODUCTS, H), 1.0, 6.0, ((0, 8),))
    w_qkv = noise(keys[3], (H, 3 * H), H ** -0.5, 0.25)
    w_out = noise(keys[4], (H, H), H ** -0.5, 0.25)
    w_msg = noise(keys[5], (H, 2 * H), H ** -0.5, 0.25)
    w_cust_up = noise(keys[6], (H, H), H ** -0.5, 0.25)
    w_prod_up = noise(keys[7], (H, H), H ** -0.5, 0.25)
    w_back = noise(keys[8], (2 * H, H), (2 * H) ** -0.5, 0.1875)
    cust_slot = with_ends(ranked(keys[9], (REVIEWS,), C_ROWS, 2), jax.random.fold_in(keys[9], 3), 0, C_ROWS - 1).astype(jnp.int32)
    prod_slot = with_ends(ranked(keys[10], (REVIEWS,), P_ROWS, 2), jax.random.fold_in(keys[10], 3), 0, P_ROWS - 1).astype(jnp.int32)
    prod_pos = jax.vmap(lambda own: jax.random.permutation(own, R_DEV))(jax.random.split(keys[11], DEVICES)).reshape((DEVICES, R_DEV)).astype(jnp.int32)
    live_count = jax.vmap(lambda own: ragged_sizes(own, N_REV * N_CUST, LIVE, CSLOT, 2))(jax.random.split(keys[12], DEVICES)).reshape((DEVICES, N_REV * N_CUST)).astype(jnp.int32)
    return {"review_cols": review_cols, "cust_state": cust_state, "prod_state": prod_state, "w_qkv": w_qkv, "w_out": w_out, "w_msg": w_msg, "w_cust_up": w_cust_up, "w_prod_up": w_prod_up, "w_back": w_back, "cust_slot": cust_slot, "prod_slot": prod_slot, "prod_pos": prod_pos, "live_count": live_count}


def rms_norm(vector):
    return vector * lax.rsqrt(lax.optimization_barrier(jnp.mean(vector * vector, axis=-1, keepdims=True)) + 1e-06)

def encode(columns, w_qkv, w_out):
    count_rows = columns.shape[0]
    column_tok = columns.reshape(count_rows * NCOL, H)
    qkv_rows = jnp.dot(column_tok, w_qkv, preferred_element_type=jnp.float32).astype(jnp.bfloat16)
    qkv_rows = qkv_rows.reshape(count_rows, NCOL, 3, HEADS, HD).astype(jnp.float32)
    queries = qkv_rows[:, :, 0]
    key_part = qkv_rows[:, :, 1]
    val_part = qkv_rows[:, :, 2]
    scores = jnp.einsum('rihd,rjhd->rhij', queries, key_part) * (1.0 / math.sqrt(HD))
    scores = scores - lax.optimization_barrier(jnp.max(scores, axis=-1, keepdims=True))
    expon = jnp.exp(scores)
    att_weight = (expon / lax.optimization_barrier(jnp.sum(expon, axis=-1, keepdims=True))).astype(jnp.bfloat16)
    attended = jnp.einsum('rhij,rjhd->rihd', att_weight.astype(jnp.float32), val_part).astype(jnp.bfloat16)
    attended = attended.reshape(count_rows * NCOL, H)
    mixed_tok = column_tok.astype(jnp.float32) + jnp.dot(attended, w_out, preferred_element_type=jnp.float32)
    pooled = lax.optimization_barrier(jnp.mean(mixed_tok.reshape(count_rows, NCOL, H), axis=1))
    return rms_norm(pooled).astype(jnp.bfloat16)

def refresh(totals, counts, states, weight):
    normed_sum = (totals / jnp.sqrt(jnp.maximum(counts, 1.0))[:, None]).astype(jnp.bfloat16)
    update = jax.nn.silu(jnp.dot(normed_sum, weight, preferred_element_type=jnp.float32))
    return rms_norm(states.astype(jnp.float32) + update).astype(jnp.bfloat16)

def reference(review_cols, cust_state, prod_state, w_qkv, w_out, w_msg, w_cust_up, w_prod_up, w_back, cust_slot, prod_slot, prod_pos, live_count):
    blocks = review_cols.reshape(DEVICES, R_DEV, NCOL * H)
    review_h = lax.map(lambda block_cols: encode(block_cols, w_qkv, w_out), blocks).reshape(REVIEWS, H)
    message = jnp.dot(review_h, w_msg, preferred_element_type=jnp.float32).astype(jnp.bfloat16)
    to_cust = message[:, :H].astype(jnp.float32)
    to_prod = message[:, H:].astype(jnp.float32)
    slot_row = jnp.arange(R_DEV, dtype=jnp.int32)
    block_of = slot_row // CSLOT
    live_rows = ((slot_row % CSLOT)[None, :] < live_count[:, block_of]).reshape(REVIEWS)
    cust_global = (block_of[None, :] * C_ROWS + cust_slot.reshape(DEVICES, R_DEV)).reshape(REVIEWS).astype(jnp.int32)
    prod_global = (prod_pos // PCAP * P_ROWS + prod_slot.reshape(DEVICES, R_DEV)).reshape(REVIEWS).astype(jnp.int32)
    live_f = live_rows.astype(jnp.float32)
    cust_sum = jax.ops.segment_sum(to_cust * live_f[:, None], cust_global, CUSTOMERS)
    cust_count = jax.ops.segment_sum(live_f, cust_global, CUSTOMERS)
    new_cust = refresh(cust_sum, cust_count, cust_state, w_cust_up)
    prod_sum = jax.ops.segment_sum(to_prod * live_f[:, None], prod_global, PRODUCTS)
    prod_count = jax.ops.segment_sum(live_f, prod_global, PRODUCTS)
    new_prod = refresh(prod_sum, prod_count, prod_state, w_prod_up)
    zero_rows = jnp.zeros((REVIEWS, H), jnp.bfloat16)
    ret_cust = jnp.where(live_rows[:, None], new_cust[cust_global], zero_rows)
    ret_prod = jnp.where(live_rows[:, None], new_prod[prod_global], zero_rows)
    back_proj = jnp.dot(jnp.concatenate([ret_cust, ret_prod], axis=1), w_back, preferred_element_type=jnp.float32)
    review_out = rms_norm(review_h.astype(jnp.float32) + back_proj).astype(jnp.bfloat16)
    return (review_out, new_cust, new_prod)
```

```python
import functools
import math

import jax
import jax.numpy as jnp
from jax import lax
from jax.experimental import pallas as pl
from jax.experimental.pallas import tpu as pltpu
from jax.sharding import PartitionSpec as P

H = 512
HEADS = 8
NCOL = 4
HD = 64
EPS = 1e-06
BF = jnp.bfloat16
F32 = jnp.float32
VMEM = pl.BlockSpec(memory_space=pltpu.VMEM)
SMEM = pl.BlockSpec(memory_space=pltpu.SMEM)
PARAMS = pltpu.CompilerParams(vmem_limit_bytes=48 * 1024 * 1024)


def rms_norm(vector):
    return vector * lax.rsqrt(jnp.mean(vector * vector, axis=-1, keepdims=True) + EPS)


def dot(left, right):
    return jnp.dot(left, right, preferred_element_type=F32)


def dot_t(left, right):
    return lax.dot_general(left, right, (((0,), (0,)), ((), ())), preferred_element_type=F32)


def one_hot(rows, first, ids):
    row = lax.broadcasted_iota(jnp.int32, (rows, ids.shape[1]), 0) + first
    return jnp.where(row == ids, 1.0, 0.0).astype(BF)


def iota(shape, dim):
    return lax.broadcasted_iota(jnp.int32, shape, dim)


def encode_rows(tokens, w_qkv, w_out, pair_sum, spread):
    rows = tokens[0].shape[0]
    stacked = jnp.concatenate(tokens, axis=0)
    qkv = dot(stacked, w_qkv).astype(BF)
    part = lambda c, which: qkv[c * rows:(c + 1) * rows, which * H:(which + 1) * H]
    lane = iota((rows, 128), 1)
    scores = jnp.zeros((rows, 128), F32)
    for j in range(NCOL):
        for i in range(NCOL):
            both = dot(part(i, 0) * part(j, 1), pair_sum)
            scores = jnp.where(lane // HEADS == j * NCOL + i, both, scores)
    scores = scores * (1.0 / math.sqrt(HD))
    top = jnp.maximum(scores, pltpu.roll(scores, 64, 1))
    top = jnp.maximum(top, pltpu.roll(top, 32, 1))
    expon = jnp.exp(scores - top)
    total = expon + pltpu.roll(expon, 64, 1)
    total = total + pltpu.roll(total, 32, 1)
    weight = (expon / total).astype(BF)
    weights = dot(weight, spread)
    attended = jnp.zeros((rows, H), F32)
    pooled = jnp.zeros((rows, H), F32)
    for j in range(NCOL):
        attended = attended + weights[:, j * H:(j + 1) * H] * part(j, 2).astype(F32)
        pooled = pooled + tokens[j].astype(F32)
    pooled = pooled + dot((attended * (1.0 / NCOL)).astype(BF), w_out) * NCOL
    return rms_norm(pooled * (1.0 / NCOL)).astype(BF)


def encode_kernel(parts, cols_ref, w_qkv_ref, w_out_ref, w_msg_ref, order_ref, h_ref, *rest):
    cust_refs, prod_refs = rest[:parts], rest[parts:2 * parts]
    held, pair_sum, spread = rest[2 * parts:]
    step = pl.program_id(0)
    rows = cols_ref.shape[0]

    @pl.when(step == 0)
    def _():
        pair_sum[...] = jnp.where(
            iota((H, 128), 0) // HD == iota((H, 128), 1) % HEADS, 1.0, 0.0
        ).astype(BF)
        lane, wide = iota((128, NCOL * H), 0), iota((128, NCOL * H), 1)
        spread[...] = jnp.where(
            (lane // (NCOL * HEADS) == wide // H) & (lane % HEADS == wide % H // HD), 1.0, 0.0
        ).astype(BF)

    tokens = [cols_ref[:, c * H:(c + 1) * H] for c in range(NCOL)]
    review_h = encode_rows(tokens, w_qkv_ref[...], w_out_ref[...], pair_sum[...], spread[...])
    h_ref[...] = review_h
    held[pl.ds(pl.multiple_of(step * rows, rows), rows), :] = review_h

    @pl.when(step == pl.num_programs(0) - 1)
    def _():
        message = dot(held[...], w_msg_ref[...]).astype(BF)
        for refs, which in ((cust_refs, 0), (prod_refs, 1)):
            for s, ref in enumerate(refs):
                size = ref.shape[0]
                pick = one_hot(size, s * size, order_ref[which:which + 1, :])
                ref[...] = dot(pick, message[:, which * H:(which + 1) * H]).astype(BF)


def encode(review_cols, w_qkv, w_out, w_msg, order, parts):
    count = review_cols.shape[0]
    rows = min(count, 128)
    piece = jax.ShapeDtypeStruct((count // parts, H), BF)
    fixed = lambda a: pl.BlockSpec(a.shape, lambda i: (0, 0))
    out = pl.pallas_call(
        functools.partial(encode_kernel, parts),
        grid=(count // rows,),
        in_specs=[pl.BlockSpec((rows, NCOL * H), lambda i: (i, 0))]
        + [fixed(a) for a in (w_qkv, w_out, w_msg, order)],
        out_specs=[pl.BlockSpec((rows, H), lambda i: (i, 0))] + [fixed(piece)] * (2 * parts),
        out_shape=[jax.ShapeDtypeStruct((count, H), BF)] + [piece] * (2 * parts),
        scratch_shapes=[
            pltpu.VMEM((count, H), BF),
            pltpu.VMEM((H, 128), BF),
            pltpu.VMEM((128, NCOL * H), BF),
        ],
        compiler_params=PARAMS,
        name="encode",
    )(review_cols, w_qkv, w_out, w_msg, order)
    return out[0], out[1:1 + parts], out[1 + parts:]


def refresh(totals, counts, states, weight):
    average = (totals / jnp.sqrt(jnp.maximum(counts, 1.0))).astype(BF)
    update = dot(average, weight)
    update = update * (1.0 / (1.0 + jnp.exp(-update)))
    return rms_norm(states.astype(F32) + update).astype(BF)


def count_of(pick):
    return jnp.sum(pick.astype(F32), axis=1, keepdims=True)


def cust_kernel(own_ref, peer_ref, ids_ref, state_ref, w_ref, new_ref, reply_ref):
    size = state_ref.shape[0]
    own = one_hot(size, 0, ids_ref[0:1, :])
    peer = one_hot(size, 0, ids_ref[1:2, :])
    totals = dot(own, own_ref[...]) + dot(peer, peer_ref[...])
    new = refresh(totals, count_of(own) + count_of(peer), state_ref[...], w_ref[...])
    new_ref[...] = new
    reply_ref[...] = dot_t(own, new).astype(BF)


def update_cust(own, peer, ids, state, weight):
    return pl.pallas_call(
        cust_kernel,
        in_specs=[VMEM] * 5,
        out_specs=[VMEM] * 2,
        out_shape=[jax.ShapeDtypeStruct(state.shape, BF), jax.ShapeDtypeStruct(own.shape, BF)],
        compiler_params=PARAMS,
        name="update_cust",
    )(own, peer, ids, state, weight)


def prod_sum_kernel(slabs, me_ref, own_ref, peer_ref, ids_ref, first_ref, *rest):
    size = first_ref.shape[0]
    rows = jnp.concatenate([own_ref[...], peer_ref[...]], axis=0)
    for t, ref in enumerate((first_ref,) + rest):
        owner = lax.rem(me_ref[0] - t + slabs, slabs)
        part = dot(one_hot(size, owner * size, ids_ref[...]), rows)
        ref[...] = part.astype(ref.dtype)


def sum_prod(me, own, peer, ids, size, slabs):
    piece = lambda kind: jax.ShapeDtypeStruct((size // slabs, H), kind)
    return pl.pallas_call(
        functools.partial(prod_sum_kernel, slabs),
        in_specs=[SMEM] + [VMEM] * 3,
        out_specs=[VMEM] * slabs,
        out_shape=[piece(F32)] + [piece(BF)] * (slabs - 1),
        compiler_params=PARAMS,
        name="sum_prod",
    )(me, own, peer, ids)


def prod_update_kernel(slabs, me_ref, ids_ref, state_ref, w_ref, *rest):
    new_ref = rest[slabs]
    size = new_ref.shape[0]
    first = pl.multiple_of(me_ref[0] * size, size)
    totals = rest[0][...]
    for ref in rest[1:slabs]:
        totals = totals + ref[...].astype(F32)
    counts = jnp.zeros((size, 1), F32)
    for r in range(ids_ref.shape[0]):
        row = iota((size, ids_ref.shape[1]), 0) + first
        counts = counts + jnp.sum(
            jnp.where(row == ids_ref[r:r + 1, :], 1.0, 0.0), axis=1, keepdims=True
        )
    new_ref[...] = refresh(totals, counts, state_ref[pl.ds(first, size), :], w_ref[...])


def update_prod(me, ids, state, weight, pieces):
    slabs = len(pieces)
    return pl.pallas_call(
        functools.partial(prod_update_kernel, slabs),
        in_specs=[SMEM] + [VMEM] * (3 + slabs),
        out_specs=VMEM,
        out_shape=jax.ShapeDtypeStruct(pieces[0].shape, BF),
        compiler_params=PARAMS,
        name="update_prod",
    )(me, ids, state, weight, *pieces)


def prod_reply_kernel(slabs, me_ref, ids_ref, *rest):
    pieces, (new_ref, own_ref, peer_ref) = rest[:slabs], rest[slabs:]
    size = pieces[0].shape[0]
    reply = None
    for t, ref in enumerate(pieces):
        first = pl.multiple_of(lax.rem(me_ref[0] + t, slabs) * size, size)
        new_ref[pl.ds(first, size), :] = ref[...]
        term = dot_t(one_hot(size, first, ids_ref[...]), ref[...])
        reply = term if reply is None else reply + term
    half = own_ref.shape[0]
    own_ref[...] = reply[:half].astype(BF)
    peer_ref[...] = reply[half:].astype(BF)


def reply_prod(me, ids, pieces):
    slabs = len(pieces)
    size, rows = pieces[0].shape[0] * slabs, ids.shape[1]
    return pl.pallas_call(
        functools.partial(prod_reply_kernel, slabs),
        in_specs=[SMEM] + [VMEM] * (1 + slabs),
        out_specs=[VMEM] * 3,
        out_shape=[jax.ShapeDtypeStruct((size, H), BF)]
        + [jax.ShapeDtypeStruct((rows // 2, H), BF)] * 2,
        compiler_params=PARAMS,
        name="reply_prod",
    )(me, ids, *pieces)


def finish_kernel(parts, order_ref, h_ref, w_ref, *rest):
    out_ref = rest[2 * parts]
    total = h_ref[...].astype(F32)
    for which in range(2):
        rows = jnp.concatenate([ref[...] for ref in rest[which * parts:(which + 1) * parts]], axis=0)
        pick = one_hot(rows.shape[0], 0, order_ref[which:which + 1, :])
        back = dot_t(pick, rows).astype(BF)
        total = total + dot(back, w_ref[which * H:(which + 1) * H, :])
    out_ref[...] = rms_norm(total).astype(BF)


def finish(order, review_h, w_back, cust_back, prod_back):
    parts = len(cust_back)
    return pl.pallas_call(
        functools.partial(finish_kernel, parts),
        in_specs=[VMEM] * (3 + 2 * parts),
        out_specs=VMEM,
        out_shape=jax.ShapeDtypeStruct(review_h.shape, BF),
        compiler_params=PARAMS,
        name="finish",
    )(order, review_h, w_back, *cust_back, *prod_back)


def shift(value, axis, by):
    size = lax.axis_size(axis)
    if by % size == 0:
        return value
    return lax.ppermute(value, axis, [(i, (i + by) % size) for i in range(size)])


def turn(array, by, axis):
    twice = jnp.concatenate([array, array], axis=axis)
    return lax.dynamic_slice_in_dim(twice, by, array.shape[axis], axis=axis)


def on_device(
    review_cols,
    cust_state,
    prod_state,
    w_qkv,
    w_out,
    w_msg,
    w_cust_up,
    w_prod_up,
    w_back,
    cust_slot,
    prod_slot,
    prod_pos,
    live_count,
):
    rows = review_cols.shape[0]
    nr, nz, nc = lax.axis_size("rev"), lax.axis_size("cust"), lax.axis_size("prod")
    mr, mz, mc = lax.axis_index("rev"), lax.axis_index("cust"), lax.axis_index("prod")
    cs = rows // (nr * nz)
    ps = rows // (nz * nc)
    me = mr.reshape(1)

    slot = jnp.arange(rows, dtype=jnp.int32)
    block = slot // cs
    position = prod_pos.reshape(rows)
    pblock = position // ps
    cust_order = (
        (mz - block % nz) % nz * (nr * cs) + (mr - block // nz) % nr * cs + slot % cs
    )
    prod_order = (
        (mz - pblock // nc) % nz * (nc * ps) + (mc - pblock % nc) % nc * ps + position % ps
    )
    order = jnp.stack([cust_order, prod_order])

    live = (slot % cs) < jnp.repeat(live_count.reshape(nr * nz), cs)
    cust_ids = jnp.where(live, cust_slot, -1)
    prod_ids = jnp.where(live, prod_slot, -1)
    prod_ids = jnp.sum(
        jnp.where(position[None, :] == slot[:, None], prod_ids[None, :], 0), axis=1
    )
    ids = lax.all_gather(jnp.stack([cust_ids, prod_ids]), ("rev", "cust", "prod"))
    ids = ids.reshape(nr, nz, nc, 2, rows)
    cust_in = lax.dynamic_slice_in_dim(ids[:, :, :, 0], (mr * nz + mz) * cs, cs, axis=3)
    cust_in = turn(turn(turn(cust_in, mr, 0), mz, 1), mc, 2)
    cust_in = cust_in.transpose(2, 0, 1, 3).reshape(nc, rows)
    prod_in = lax.dynamic_slice_in_dim(ids[:, :, :, 1], (mz * nc + mc) * ps, ps, axis=3)
    prod_all = prod_in.reshape(nr, rows)
    prod_in = lax.dynamic_index_in_dim(prod_in, mr, 0, keepdims=False)
    prod_in = turn(turn(prod_in, mz, 0), mc, 1).transpose(1, 0, 2).reshape(1, rows)

    review_h, cust_parts, prod_parts = encode(review_cols, w_qkv, w_out, w_msg, order, nz)

    prod_got = [shift(prod_parts[s], "cust", -s) for s in range(nz)]
    own = jnp.concatenate([p[:ps] for p in prod_got], axis=0)
    peer = shift(jnp.concatenate([p[ps:] for p in prod_got], axis=0), "prod", -1)
    pieces = sum_prod(me, own, peer, prod_in, prod_state.shape[0], nr)
    pieces = [shift(pieces[t], "rev", -t) for t in range(nr)]
    new_piece = update_prod(me, prod_all, prod_state, w_prod_up, pieces)
    new_pieces = [shift(new_piece, "rev", -t) for t in range(nr)]
    new_prod, own_reply, peer_reply = reply_prod(me, prod_in, new_pieces)
    peer_reply = shift(peer_reply, "prod", 1)
    prod_back = [
        shift(
            jnp.concatenate([own_reply[s * ps:(s + 1) * ps], peer_reply[s * ps:(s + 1) * ps]]),
            "cust",
            s,
        )
        for s in range(nz)
    ]

    cust_got = [shift(cust_parts[s], "cust", -s) for s in range(nz)]
    cust_got = [
        shift(jnp.concatenate([p[t * cs:(t + 1) * cs] for p in cust_got], axis=0), "rev", -t)
        for t in range(nr)
    ]
    own = jnp.concatenate(cust_got, axis=0)
    new_cust, reply = update_cust(own, shift(own, "prod", -1), cust_in, cust_state, w_cust_up)
    size = nz * cs
    reply = [shift(reply[t * size:(t + 1) * size], "rev", t) for t in range(nr)]
    cust_back = [
        shift(jnp.concatenate([p[s * cs:(s + 1) * cs] for p in reply], axis=0), "cust", s)
        for s in range(nz)
    ]

    review_out = finish(order, review_h, w_back, cust_back, prod_back)
    return (review_out, new_cust, new_prod)


def solution(mesh):
    every = P(("rev", "cust", "prod"))
    in_specs = (
        P(("rev", "cust", "prod"), None),
        P(("rev", "cust"), None),
        P(("cust", "prod"), None),
        P(),
        P(),
        P(),
        P(),
        P(),
        P(),
        every,
        every,
        P(("rev", "cust", "prod"), None),
        P(("rev", "cust", "prod"), None),
    )
    out_specs = (
        P(("rev", "cust", "prod"), None),
        P(("rev", "cust"), None),
        P(("cust", "prod"), None),
    )
    return jax.shard_map(
        on_device, mesh=mesh, in_specs=in_specs, out_specs=out_specs, check_vma=False
    )
```

```python
import functools
import math

import jax
import jax.numpy as jnp
from jax import lax
from jax.experimental import pallas as pl
from jax.experimental.pallas import tpu as pltpu
from jax.sharding import PartitionSpec as P

H = 512
HEADS = 8
NCOL = 4
HD = 64
EPS = 1e-06
BF = jnp.bfloat16
F32 = jnp.float32
ID_ROWS = 16
VMEM = pl.BlockSpec(memory_space=pltpu.VMEM)
HBM = pl.BlockSpec(memory_space=pl.ANY)
SMEM = pl.BlockSpec(memory_space=pltpu.SMEM)
PARAMS = pltpu.CompilerParams(vmem_limit_bytes=48 * 1024 * 1024)


def rms_norm(vector):
    return vector * lax.rsqrt(jnp.mean(vector * vector, axis=-1, keepdims=True) + EPS)


def dot(left, right):
    return jnp.dot(left, right, preferred_element_type=F32)


def dot_t(left, right):
    return lax.dot_general(left, right, (((0,), (0,)), ((), ())), preferred_element_type=F32)


def dot_nt(left, right):
    return lax.dot_general(left, right, (((1,), (1,)), ((), ())), preferred_element_type=F32)


def one_hot(rows, first, ids):
    row = lax.broadcasted_iota(jnp.int32, (rows, ids.shape[1]), 0) + first
    return jnp.where(row == ids, 1.0, 0.0).astype(BF)


def iota(shape, dim):
    return lax.broadcasted_iota(jnp.int32, shape, dim)


def encode_rows(tokens, w_qkv, w_out, pair_sum, spread, before):
    rows = tokens[0].shape[0]
    stacked = jnp.concatenate(tokens, axis=0)
    part = []
    for which in range(3):
        before(which)
        made = dot(stacked, w_qkv[:, which * H:(which + 1) * H]).astype(BF)
        part.append([made[c * rows:(c + 1) * rows] for c in range(NCOL)])
    query, key, value = part
    lane = iota((rows, 128), 1)
    scores = jnp.zeros((rows, 128), F32)
    for j in range(NCOL):
        both = dot(jnp.concatenate([query[i] * key[j] for i in range(NCOL)], axis=0), pair_sum)
        for i in range(NCOL):
            scores = jnp.where(lane >> 3 == j * NCOL + i, both[i * rows:(i + 1) * rows], scores)
    scores = scores * (1.0 / math.sqrt(HD))
    top = jnp.maximum(scores, pltpu.roll(scores, 64, 1))
    top = jnp.maximum(top, pltpu.roll(top, 32, 1))
    expon = jnp.exp(scores - top)
    total = expon + pltpu.roll(expon, 64, 1)
    total = total + pltpu.roll(total, 32, 1)
    weight = (expon / total).astype(BF).astype(F32)
    attended = jnp.zeros((rows, H), F32)
    pooled = jnp.zeros((rows, H), F32)
    for j in range(NCOL):
        turned = pltpu.roll(weight, (128 - NCOL * HEADS * j) % 128, 1).astype(BF)
        attended = attended + dot(turned, spread) * value[j].astype(F32)
        pooled = pooled + tokens[j].astype(F32)
    before(3)
    mixed = dot((attended * (1.0 / NCOL)).astype(BF), w_out[...])
    return rms_norm(pooled * (1.0 / NCOL) + mixed).astype(BF)


def split_ids(ids):
    row = iota((ID_ROWS, ids.shape[1]), 0)
    halves = jnp.where(row == 0, ids >> 5, jnp.where(row == 1, ids & 31, 0))
    return halves.astype(F32).astype(BF)


def encode_kernel(parts, rows, x_hbm, w_qkv_hbm, w_out_hbm, w_msg_hbm, order_ref, h_ref, *rest):
    cust_refs, prod_refs = rest[:parts], rest[parts:2 * parts]
    x_ref, w_qkv, w_out, w_msg, sem = rest[2 * parts:]
    chunks = x_hbm.shape[0] // rows
    copy = pltpu.make_async_copy
    x_copies = [
        copy(x_hbm.at[pl.ds(c * rows, rows)], x_ref.at[pl.ds(c * rows, rows)], sem.at[c])
        for c in range(chunks)
    ]
    w_copies = [
        copy(w_qkv_hbm.at[:, pl.ds(k * H, H)], w_qkv.at[:, pl.ds(k * H, H)], sem.at[chunks + k])
        for k in range(3)
    ]
    w_copies.append(copy(w_out_hbm, w_out, sem.at[chunks + 3]))
    last = copy(w_msg_hbm, w_msg, sem.at[chunks + 4])
    x_copies[0].start()
    w_copies[0].start()
    w_copies[1].start()
    pair_sum = jnp.where(iota((H, 128), 0) >> 6 == (iota((H, 128), 1) & 7), 1.0, 0.0).astype(BF)
    spread = jnp.where(
        (iota((128, H), 0) < NCOL * HEADS) & ((iota((128, H), 0) & 7) == iota((128, H), 1) >> 6),
        1.0,
        0.0,
    ).astype(BF)

    def first_before(which):
        w_copies[which].wait()
        if which == 0:
            w_copies[2].start()
            for x_copy in x_copies[1:]:
                x_copy.start()
        if which == 1:
            w_copies[3].start()
            last.start()

    for c in range(chunks):
        x_copies[c].wait()
        at = slice(c * rows, (c + 1) * rows)
        tokens = [x_ref[at, k * H:(k + 1) * H] for k in range(NCOL)]
        before = first_before if c == 0 else lambda which: None
        h_ref[at, :] = encode_rows(tokens, w_qkv, w_out, pair_sum, spread, before)
    last.wait()
    message = dot(h_ref[...], w_msg[...]).astype(BF)
    for refs, which in ((cust_refs, 0), (prod_refs, 1)):
        ids = split_ids(order_ref[2 + which:3 + which, :])
        for s, ref in enumerate(refs):
            size = ref.shape[0] - ID_ROWS
            pick = one_hot(size, s * size, order_ref[which:which + 1, :])
            ref[:size, :] = dot(pick, message[:, which * H:(which + 1) * H]).astype(BF)
            ref[size:, :] = jnp.zeros((ID_ROWS, H), BF)
            ref[size:, :size] = dot_nt(ids, pick).astype(BF)


def encode(review_cols, w_qkv, w_out, w_msg, order, parts):
    count = review_cols.shape[0]
    rows = min(count, 256)
    piece = jax.ShapeDtypeStruct((count // parts + ID_ROWS, H), BF)
    out = pl.pallas_call(
        functools.partial(encode_kernel, parts, rows),
        in_specs=[HBM] * 4 + [VMEM],
        out_specs=[VMEM] * (1 + 2 * parts),
        out_shape=[jax.ShapeDtypeStruct((count, H), BF)] + [piece] * (2 * parts),
        scratch_shapes=[pltpu.VMEM(a.shape, BF) for a in (review_cols, w_qkv, w_out, w_msg)]
        + [pltpu.SemaphoreType.DMA((count // rows + 5,))],
        compiler_params=PARAMS,
        name="encode",
    )(review_cols, w_qkv, w_out, w_msg, order)
    return out[0], out[1:1 + parts], out[1 + parts:]


def refresh(totals, counts, states, weight):
    average = (totals / jnp.sqrt(jnp.maximum(counts, 1.0))).astype(BF)
    update = dot(average, weight)
    update = update * (1.0 / (1.0 + jnp.exp(-update)))
    return rms_norm(states.astype(F32) + update).astype(BF)


def count_of(pick):
    return jnp.sum(pick.astype(F32), axis=1, keepdims=True)


def cust_kernel(groups, own_ref, peer_ref, ids_ref, state_ref, w_ref, new_ref, reply_ref):
    size = state_ref.shape[0]
    held = own_ref.shape[0] // groups
    totals, counts = jnp.zeros((size, H), F32), jnp.zeros((size, 1), F32)
    for which, ref in ((1, peer_ref), (0, own_ref)):
        rows = jnp.concatenate(
            [ref[t * held:(t + 1) * held - ID_ROWS, :] for t in range(groups)], axis=0
        )
        pick = one_hot(size, 0, ids_ref[which:which + 1, :])
        totals = totals + dot(pick, rows)
        counts = counts + count_of(pick)
    new = refresh(totals, counts, state_ref[...], w_ref[...])
    new_ref[...] = new
    reply_ref[...] = dot_t(pick, new).astype(BF)


def update_cust(groups, own, peer, ids, state, weight):
    return pl.pallas_call(
        functools.partial(cust_kernel, groups),
        in_specs=[VMEM] * 5,
        out_specs=[VMEM] * 2,
        out_shape=[
            jax.ShapeDtypeStruct(state.shape, BF),
            jax.ShapeDtypeStruct((ids.shape[1], H), BF),
        ],
        compiler_params=PARAMS,
        name="update_cust",
    )(own, peer, ids, state, weight)


def prod_sum_kernel(slabs, me_ref, own_ref, peer_ref, ids_ref, *pieces):
    size = pieces[0].shape[0] - ID_ROWS
    rows = jnp.concatenate([own_ref[...], peer_ref[:own_ref.shape[0], :]], axis=0)
    ones = jnp.ones((ID_ROWS, rows.shape[0]), BF)
    row = iota((ID_ROWS, size), 0)
    for t, ref in enumerate(pieces):
        owner = lax.rem(me_ref[0] - t + slabs, slabs)
        pick = one_hot(size, owner * size, ids_ref[...])
        counts = dot_nt(ones, pick).astype(jnp.int32)
        halves = jnp.where(row == 0, counts >> 5, jnp.where(row == 1, counts & 31, 0))
        ref[:size, :] = dot(pick, rows).astype(ref.dtype)
        ref[size:, :] = jnp.zeros((ID_ROWS, H), ref.dtype)
        ref[size:, :size] = halves.astype(F32).astype(ref.dtype)


def sum_prod(me, own, peer, ids, size, slabs):
    piece = lambda kind: jax.ShapeDtypeStruct((size // slabs + ID_ROWS, H), kind)
    return pl.pallas_call(
        functools.partial(prod_sum_kernel, slabs),
        in_specs=[SMEM] + [VMEM] * 3,
        out_specs=[VMEM] * slabs,
        out_shape=[piece(F32)] + [piece(BF)] * (slabs - 1),
        compiler_params=PARAMS,
        name="sum_prod",
    )(me, own, peer, ids)


def prod_update_kernel(slabs, me_ref, state_ref, w_ref, *rest):
    new_ref = rest[slabs]
    size = new_ref.shape[0]
    first = pl.multiple_of(me_ref[0] * size, size)
    totals = sum(ref[:size, :].astype(F32) for ref in rest[:slabs])
    halves = sum(ref[size:, :size].astype(F32) for ref in rest[:slabs])
    count_row = halves[0:1, :] * 32.0 + halves[1:2, :]
    diagonal = iota((size, size), 0) == iota((size, size), 1)
    counts = jnp.sum(jnp.where(diagonal, count_row, 0.0), axis=1, keepdims=True)
    new_ref[...] = refresh(totals, counts, state_ref[pl.ds(first, size), :], w_ref[...])


def update_prod(me, state, weight, pieces):
    slabs = len(pieces)
    return pl.pallas_call(
        functools.partial(prod_update_kernel, slabs),
        in_specs=[SMEM] + [VMEM] * (2 + slabs),
        out_specs=VMEM,
        out_shape=jax.ShapeDtypeStruct((state.shape[0] // slabs, H), BF),
        compiler_params=PARAMS,
        name="update_prod",
    )(me, state, weight, *pieces)


def prod_reply_kernel(slabs, me_ref, ids_ref, *rest):
    pieces, (new_ref, own_ref, peer_ref) = rest[:slabs], rest[slabs:]
    size = pieces[0].shape[0]
    reply = None
    for t, ref in enumerate(pieces):
        first = pl.multiple_of(lax.rem(me_ref[0] + t, slabs) * size, size)
        new_ref[pl.ds(first, size), :] = ref[...]
        term = dot_t(one_hot(size, first, ids_ref[...]), ref[...])
        reply = term if reply is None else reply + term
    half = own_ref.shape[0]
    own_ref[...] = reply[:half].astype(BF)
    peer_ref[...] = reply[half:].astype(BF)


def reply_prod(me, ids, pieces):
    slabs = len(pieces)
    size, rows = pieces[0].shape[0] * slabs, ids.shape[1]
    return pl.pallas_call(
        functools.partial(prod_reply_kernel, slabs),
        in_specs=[SMEM] + [VMEM] * (1 + slabs),
        out_specs=[VMEM] * 3,
        out_shape=[jax.ShapeDtypeStruct((size, H), BF)]
        + [jax.ShapeDtypeStruct((rows // 2, H), BF)] * 2,
        compiler_params=PARAMS,
        name="reply_prod",
    )(me, ids, *pieces)


def finish_kernel(parts, order_ref, h_ref, w_ref, *rest):
    out_ref = rest[2 * parts]
    total = h_ref[...].astype(F32)
    for which in range(2):
        rows = jnp.concatenate([ref[...] for ref in rest[which * parts:(which + 1) * parts]], axis=0)
        pick = one_hot(rows.shape[0], 0, order_ref[which:which + 1, :])
        back = dot_t(pick, rows).astype(BF)
        total = total + dot(back, w_ref[which * H:(which + 1) * H, :])
    out_ref[...] = rms_norm(total).astype(BF)


def finish(order, review_h, w_back, cust_back, prod_back):
    parts = len(cust_back)
    return pl.pallas_call(
        functools.partial(finish_kernel, parts),
        in_specs=[VMEM] * (3 + 2 * parts),
        out_specs=VMEM,
        out_shape=jax.ShapeDtypeStruct(review_h.shape, BF),
        compiler_params=PARAMS,
        name="finish",
    )(order, review_h, w_back, *cust_back, *prod_back)


def shift(value, axis, by):
    size = lax.axis_size(axis)
    if by % size == 0:
        return value
    return lax.ppermute(value, axis, [(i, (i + by) % size) for i in range(size)])


def read_ids(rows):
    rows = rows[:2].astype(F32)
    return (rows[0:1] * 32.0 + rows[1:2]).astype(jnp.int32) - 1


def with_ids(rows, ids):
    return jnp.concatenate([rows, jnp.pad(ids, ((0, 0), (0, H - ids.shape[1])))], axis=0)


def on_device(
    review_cols,
    cust_state,
    prod_state,
    w_qkv,
    w_out,
    w_msg,
    w_cust_up,
    w_prod_up,
    w_back,
    cust_slot,
    prod_slot,
    prod_pos,
    live_count,
):
    rows = review_cols.shape[0]
    nr, nz, nc = lax.axis_size("rev"), lax.axis_size("cust"), lax.axis_size("prod")
    mr, mz, mc = lax.axis_index("rev"), lax.axis_index("cust"), lax.axis_index("prod")
    cs = rows // (nr * nz)
    ps = rows // (nz * nc)
    me = mr.reshape(1)

    slot = jnp.arange(rows, dtype=jnp.int32)
    block = slot // cs
    position = prod_pos.reshape(rows)
    pblock = position // ps
    cust_order = (
        (mz - block % nz) % nz * (nr * cs) + (mr - block // nz) % nr * cs + slot % cs
    )
    prod_order = (
        (mz - pblock // nc) % nz * (nc * ps) + (mc - pblock % nc) % nc * ps + position % ps
    )
    live = (slot % cs) < jnp.repeat(live_count.reshape(nr * nz), cs)
    order = jnp.stack(
        [
            cust_order,
            prod_order,
            jnp.where(live, cust_slot + 1, 0),
            jnp.where(live, prod_slot + 1, 0),
        ]
    )
    review_h, cust_parts, prod_parts = encode(review_cols, w_qkv, w_out, w_msg, order, nz)

    got = [shift(prod_parts[s], "cust", -s) for s in range(nz)]
    half = lambda u: jnp.concatenate([p[u * ps:(u + 1) * ps] for p in got], axis=0)
    half_ids = lambda u: jnp.concatenate(
        [p[nc * ps:, u * ps:(u + 1) * ps] for p in got], axis=1
    )
    own, peer = half(0), shift(with_ids(half(1), half_ids(1)), "prod", -1)
    prod_in = jnp.concatenate(
        [read_ids(half_ids(0)), read_ids(peer[nz * ps:, :nz * ps])], axis=1
    )
    pieces = sum_prod(me, own, peer, prod_in, prod_state.shape[0], nr)
    pieces = [shift(pieces[t], "rev", -t) for t in range(nr)]
    new_piece = update_prod(me, prod_state, w_prod_up, pieces)
    new_pieces = [shift(new_piece, "rev", -t) for t in range(nr)]
    new_prod, own_reply, peer_reply = reply_prod(me, prod_in, new_pieces)
    peer_reply = shift(peer_reply, "prod", 1)
    prod_back = [
        shift(
            jnp.concatenate([own_reply[s * ps:(s + 1) * ps], peer_reply[s * ps:(s + 1) * ps]]),
            "cust",
            s,
        )
        for s in range(nz)
    ]

    got = [shift(cust_parts[s], "cust", -s) for s in range(nz)]
    group = lambda t: jnp.concatenate([p[t * cs:(t + 1) * cs] for p in got], axis=0)
    group_ids = lambda t: jnp.concatenate(
        [p[nr * cs:, t * cs:(t + 1) * cs] for p in got], axis=1
    )
    got_groups = [shift(with_ids(group(t), group_ids(t)), "rev", -t) for t in range(nr)]
    own = jnp.concatenate(got_groups, axis=0)
    peer = shift(own, "prod", -1)
    size = nz * cs
    held = size + ID_ROWS
    cust_in = jnp.concatenate(
        [
            jnp.concatenate(
                [read_ids(a[t * held + size:(t + 1) * held, :size]) for t in range(nr)], axis=1
            )
            for a in (own, peer)
        ],
        axis=0,
    )
    new_cust, reply = update_cust(nr, own, peer, cust_in, cust_state, w_cust_up)
    reply = [shift(reply[t * size:(t + 1) * size], "rev", t) for t in range(nr)]
    cust_back = [
        shift(jnp.concatenate([p[s * cs:(s + 1) * cs] for p in reply], axis=0), "cust", s)
        for s in range(nz)
    ]

    review_out = finish(order, review_h, w_back, cust_back, prod_back)
    return (review_out, new_cust, new_prod)


def solution(mesh):
    every = P(("rev", "cust", "prod"))
    in_specs = (
        P(("rev", "cust", "prod"), None),
        P(("rev", "cust"), None),
        P(("cust", "prod"), None),
        P(),
        P(),
        P(),
        P(),
        P(),
        P(),
        every,
        every,
        P(("rev", "cust", "prod"), None),
        P(("rev", "cust", "prod"), None),
    )
    out_specs = (
        P(("rev", "cust", "prod"), None),
        P(("rev", "cust"), None),
        P(("cust", "prod"), None),
    )
    return jax.shard_map(
        on_device, mesh=mesh, in_specs=in_specs, out_specs=out_specs, check_vma=False
    )
```

```python
import functools
import math

import jax
import jax.numpy as jnp
from jax import lax
from jax.experimental import pallas as pl
from jax.experimental.pallas import tpu as pltpu
from jax.sharding import PartitionSpec as P

H = 512
HEADS = 8
NCOL = 4
HD = 64
EPS = 1e-06
BF = jnp.bfloat16
F32 = jnp.float32
ID_ROWS = 16
VMEM = pl.BlockSpec(memory_space=pltpu.VMEM)
HBM = pl.BlockSpec(memory_space=pltpu.HBM)
ANY = pl.BlockSpec(memory_space=pl.ANY)
SMEM = pl.BlockSpec(memory_space=pltpu.SMEM)
PARAMS = pltpu.CompilerParams(vmem_limit_bytes=16 * 1024 * 1024)
ENCODE_PARAMS = pltpu.CompilerParams(vmem_limit_bytes=60 * 1024 * 1024)


def rms_norm(vector):
    return vector * lax.rsqrt(jnp.mean(vector * vector, axis=-1, keepdims=True) + EPS)


def dot(left, right):
    return jnp.dot(left, right, preferred_element_type=F32)


def dot_t(left, right):
    return lax.dot_general(left, right, (((0,), (0,)), ((), ())), preferred_element_type=F32)


def dot_nt(left, right):
    return lax.dot_general(left, right, (((1,), (1,)), ((), ())), preferred_element_type=F32)


def one_hot(rows, first, ids):
    row = lax.broadcasted_iota(jnp.int32, (rows, ids.shape[1]), 0) + first
    return jnp.where(row == ids, 1.0, 0.0).astype(BF)


def iota(shape, dim):
    return lax.broadcasted_iota(jnp.int32, shape, dim)


def encode_rows(tokens, w_qkv, w_out, pair_sum, spread, before):
    rows = tokens[0].shape[0]
    stacked = jnp.concatenate(tokens, axis=0)
    part = []
    for which in range(3):
        before(which)
        made = dot(stacked, w_qkv[:, which * H:(which + 1) * H]).astype(BF)
        part.append([made[c * rows:(c + 1) * rows] for c in range(NCOL)])
    query, key, value = part
    lane = iota((rows, 128), 1)
    scores = jnp.zeros((rows, 128), F32)
    for j in range(NCOL):
        both = dot(jnp.concatenate([query[i] * key[j] for i in range(NCOL)], axis=0), pair_sum)
        for i in range(NCOL):
            scores = jnp.where(lane >> 3 == j * NCOL + i, both[i * rows:(i + 1) * rows], scores)
    scores = scores * (1.0 / math.sqrt(HD))
    top = jnp.maximum(scores, pltpu.roll(scores, 64, 1))
    top = jnp.maximum(top, pltpu.roll(top, 32, 1))
    expon = jnp.exp(scores - top)
    total = expon + pltpu.roll(expon, 64, 1)
    total = total + pltpu.roll(total, 32, 1)
    weight = (expon / total).astype(BF).astype(F32)
    attended = jnp.zeros((rows, H), F32)
    pooled = jnp.zeros((rows, H), F32)
    for j in range(NCOL):
        turned = pltpu.roll(weight, (128 - NCOL * HEADS * j) % 128, 1).astype(BF)
        attended = attended + dot(turned, spread) * value[j].astype(F32)
        pooled = pooled + tokens[j].astype(F32)
    before(3)
    mixed = dot((attended * (1.0 / NCOL)).astype(BF), w_out[...])
    return rms_norm(pooled * (1.0 / NCOL) + mixed).astype(BF)


def halves_at(ids, place, count):
    row = iota((count, ids.shape[1]), 0)
    halves = jnp.where((row & 1) == 0, ids >> 5, ids & 31)
    return jnp.where(row >> 1 == place, halves, 0).astype(F32).astype(BF)


def id_rows(count):
    return -(-2 * count // ID_ROWS) * ID_ROWS


def split(index, size):
    if size & (size - 1) == 0:
        return index >> (size.bit_length() - 1), index & (size - 1)
    return lax.div(index, size), lax.rem(index, size)


def send_orders(sizes, me_ref, pos, cust_slot, prod_slot, live_ref):
    nr, nz, nc = sizes
    rows = pos.shape[1]
    cs, ps = rows // (nr * nz), rows // (nz * nc)
    mr, mz, mc = me_ref[0], me_ref[1], me_ref[2]
    block, k = split(iota((1, rows), 1), cs)
    r, z = split(block, nz)
    live = jnp.zeros((1, rows), jnp.int32)
    for b in range(nr * nz):
        live = jnp.where(block == b, live_ref[0, b], live)
    cust = mz ^ z, mr ^ r, k, jnp.where(k < live, cust_slot + 1, 0)
    prod_id = jnp.where(k < live, prod_slot + 1, 0)
    block, k = split(pos, ps)
    z, c = split(block, nc)
    return cust, (mz ^ z, mc ^ c, k, prod_id)


def encode_kernel(sizes, rows, *refs):
    x_hbm, w_qkv_hbm, w_out_hbm, w_msg_hbm, me_ref = refs[:5]
    index_hbm, (h_ref, order_ref) = refs[5:9], refs[9:11]
    x_ref, w_qkv, w_out, w_msg, pos_ref, cust_slot_ref, prod_slot_ref, live_ref, sem = refs[-9:]
    nr, nz, nc = sizes
    cust_refs, prod_refs = refs[11:11 + nz], refs[11 + nz:-9]
    chunks = x_hbm.shape[0] // rows
    copy = pltpu.make_async_copy
    x_copies = [
        copy(x_hbm.at[pl.ds(c * rows, rows)], x_ref.at[pl.ds(c * rows, rows)], sem.at[c])
        for c in range(chunks)
    ]
    w_copies = [
        copy(w_qkv_hbm.at[:, pl.ds(k * H, H)], w_qkv.at[:, pl.ds(k * H, H)], sem.at[chunks + k])
        for k in range(3)
    ]
    w_copies.append(copy(w_out_hbm, w_out, sem.at[chunks + 3]))
    last = copy(w_msg_hbm, w_msg, sem.at[chunks + 4])
    index_refs = (pos_ref, cust_slot_ref, prod_slot_ref, live_ref)
    index_copies = [
        copy(source, ref, sem.at[chunks + 5 + n])
        for n, (source, ref) in enumerate(zip(index_hbm, index_refs))
    ]
    x_copies[0].start()
    w_copies[0].start()
    w_copies[1].start()
    for index_copy in index_copies:
        index_copy.start()
    pair_sum = jnp.where(iota((H, 128), 0) >> 6 == (iota((H, 128), 1) & 7), 1.0, 0.0).astype(BF)
    spread = jnp.where(
        (iota((128, H), 0) < NCOL * HEADS) & ((iota((128, H), 0) & 7) == iota((128, H), 1) >> 6),
        1.0,
        0.0,
    ).astype(BF)

    def first_before(which):
        w_copies[which].wait()
        if which == 0:
            w_copies[2].start()
            for x_copy in x_copies[1:]:
                x_copy.start()
        if which == 1:
            w_copies[3].start()
            last.start()

    for c in range(chunks):
        x_copies[c].wait()
        at = slice(c * rows, (c + 1) * rows)
        tokens = [x_ref[at, k * H:(k + 1) * H] for k in range(NCOL)]
        before = first_before if c == 0 else lambda which: None
        h_ref[at, :] = encode_rows(tokens, w_qkv, w_out, pair_sum, spread, before)
    for index_copy in index_copies:
        index_copy.wait()
    (s_of, t_of, k, ids), (ps_of, u_of, pk, prod_ids) = send_orders(
        sizes, me_ref, pos_ref[...], cust_slot_ref[...], prod_slot_ref[...], live_ref
    )
    count = h_ref.shape[0]
    cs, ps = count // (nr * nz), count // (nz * nc)
    cust_sent, prod_sent = (s_of * nr + t_of) * cs + k, (u_of * nz + ps_of) * ps + pk
    order_ref[0:1, :] = (t_of * nz + s_of) * cs + k
    order_ref[1:2, :] = prod_sent
    lanes = one_hot(nz * cs, 0, s_of * cs + k)
    halves = halves_at(ids, t_of, id_rows(nr))
    cust_ids = [
        dot_nt(jnp.where(s_of == s, halves, jnp.zeros_like(halves)), lanes) for s in range(nz)
    ]
    lanes = one_hot(nc * ps, 0, u_of * ps + pk)
    halves = halves_at(prod_ids, ps_of * (ID_ROWS // 2), nz * ID_ROWS)
    prod_ids = [
        dot_nt(jnp.where(u_of == u, halves, jnp.zeros_like(halves)), lanes) for u in range(nc)
    ]
    last.wait()
    message = dot(h_ref[...], w_msg[...]).astype(BF)
    for sent, made, refs, which in (
        (cust_sent, cust_ids, cust_refs, 0),
        (prod_sent, prod_ids, prod_refs, 1),
    ):
        size = count // len(refs)
        for s, ref in enumerate(refs):
            pick = one_hot(size, s * size, sent)
            ref[:size, :] = dot(pick, message[:, which * H:(which + 1) * H]).astype(BF)
            ref[size:, :] = jnp.zeros((ref.shape[0] - size, H), BF)
            ref[size:, :made[s].shape[1]] = made[s].astype(BF)


def encode(sizes, me, review_cols, w_qkv, w_out, w_msg, *index):
    count = review_cols.shape[0]
    nr, nz, nc = sizes
    rows = min(count, 256)
    cust_block = jax.ShapeDtypeStruct((count // nz + id_rows(nr), H), BF)
    prod_block = jax.ShapeDtypeStruct((count // nc + nz * ID_ROWS, H), BF)
    out = pl.pallas_call(
        functools.partial(encode_kernel, sizes, rows),
        in_specs=[HBM] * 4 + [SMEM] + [HBM] * 4,
        out_specs=[VMEM] * (2 + nz + nc),
        out_shape=[
            jax.ShapeDtypeStruct((count, H), BF),
            jax.ShapeDtypeStruct((2, count), jnp.int32),
        ]
        + [cust_block] * nz
        + [prod_block] * nc,
        scratch_shapes=[pltpu.VMEM(a.shape, BF) for a in (review_cols, w_qkv, w_out, w_msg)]
        + [pltpu.VMEM(a.shape, jnp.int32) for a in index[:3]]
        + [pltpu.SMEM(index[3].shape, jnp.int32)]
        + [pltpu.SemaphoreType.DMA((count // rows + 9,))],
        compiler_params=ENCODE_PARAMS,
        name="encode",
    )(review_cols, w_qkv, w_out, w_msg, me, *index)
    return out[0], out[1], out[2:2 + nz], out[2 + nz:]


def pair_kernel(parts, own_ref, peer_ref, *refs):
    part = (own_ref.shape[0] - parts * ID_ROWS) // parts
    for s, ref in enumerate(refs[-parts:]):
        at = parts * part + s * ID_ROWS
        ref[:part, :] = own_ref[s * part:(s + 1) * part, :]
        ref[part:2 * part, :] = peer_ref[s * part:(s + 1) * part, :]
        ref[2 * part:, :] = own_ref[at:at + ID_ROWS, :] + peer_ref[at:at + ID_ROWS, :]


def pair(parts, own, peer, after):
    part = (own.shape[0] - parts * ID_ROWS) // parts
    return pl.pallas_call(
        functools.partial(pair_kernel, parts),
        in_specs=[VMEM] * 2 + [ANY] * len(after),
        out_specs=[VMEM] * parts,
        out_shape=[jax.ShapeDtypeStruct((2 * part + ID_ROWS, H), BF)] * parts,
        compiler_params=PARAMS,
        name="pair_product_blocks",
    )(own, peer, *after)


def regroup_kernel(size, parts, groups, *refs):
    held = groups * size
    for t, ref in enumerate(refs[-groups:]):
        for s in range(parts):
            ref[s * size:(s + 1) * size, :] = refs[s][t * size:(t + 1) * size, :]
        ref[parts * size:, :] = sum(refs[s][held:, :] for s in range(parts))


def regroup(size, groups, got, after):
    parts, ids = len(got), got[0].shape[0] - groups * size
    if size % 16:
        tail = sum(p[groups * size:] for p in got)
        return [
            jnp.concatenate([p[t * size:(t + 1) * size] for p in got] + [tail], axis=0)
            for t in range(groups)
        ]
    return pl.pallas_call(
        functools.partial(regroup_kernel, size, parts, groups),
        in_specs=[VMEM] * parts + [ANY] * len(after),
        out_specs=[VMEM] * groups,
        out_shape=[jax.ShapeDtypeStruct((parts * size + ids, H), BF)] * groups,
        compiler_params=PARAMS,
        name="regroup_customer_blocks",
    )(*got, *after)


def join_kernel(count, *refs):
    at = 0
    for ref in refs[:count]:
        refs[-1][at:at + ref.shape[0], :] = ref[...]
        at += ref.shape[0]


def join(parts, after):
    rows = sum(part.shape[0] for part in parts)
    return pl.pallas_call(
        functools.partial(join_kernel, len(parts)),
        in_specs=[VMEM] * len(parts) + [ANY] * len(after),
        out_specs=VMEM,
        out_shape=jax.ShapeDtypeStruct((rows, H), BF),
        compiler_params=PARAMS,
        name="join",
    )(*parts, *after)


def refresh(totals, counts, states, weight):
    average = (totals / jnp.sqrt(jnp.maximum(counts, 1.0))).astype(BF)
    update = dot(average, weight)
    update = update * (1.0 / (1.0 + jnp.exp(-update)))
    return rms_norm(states.astype(F32) + update).astype(BF)


def count_of(pick):
    return jnp.sum(pick.astype(F32), axis=1, keepdims=True)


def ids_in(rows):
    rows = rows.astype(F32)
    return (rows[0:1, :] * 32.0 + rows[1:2, :]).astype(jnp.int32) - 1


def cust_kernel(groups, own_ref, peer_ref, state_ref, w_ref, *refs):
    new_ref, reply_ref = refs[-2:]
    size = state_ref.shape[0]
    held = own_ref.shape[0] // groups
    rows = held - id_rows(groups)
    totals, counts = jnp.zeros((size, H), F32), jnp.zeros((size, 1), F32)
    for ref in (peer_ref, own_ref):
        ids = [
            ids_in(ref[t * held + rows:(t + 1) * held, :rows][2 * t:2 * t + 2, :])
            for t in range(groups)
        ]
        pick = one_hot(size, 0, jnp.concatenate(ids, axis=1))
        messages = [ref[t * held:t * held + rows, :] for t in range(groups)]
        totals = totals + dot(pick, jnp.concatenate(messages, axis=0))
        counts = counts + count_of(pick)
    new = refresh(totals, counts, state_ref[...], w_ref[...])
    new_ref[...] = new
    reply_ref[...] = dot_t(pick, new).astype(BF)


def update_cust(groups, own, peer, state, weight, after):
    rows = own.shape[0] - groups * id_rows(groups)
    return pl.pallas_call(
        functools.partial(cust_kernel, groups),
        in_specs=[VMEM] * 4 + [ANY] * len(after),
        out_specs=[VMEM] * 2,
        out_shape=[
            jax.ShapeDtypeStruct(state.shape, BF),
            jax.ShapeDtypeStruct((rows, H), BF),
        ],
        compiler_params=PARAMS,
        name="update_cust",
    )(own, peer, state, weight, *after)


def prod_sum_kernel(slabs, parts, me_ref, ids_ref, *refs):
    blocks, pieces = refs[:parts], refs[-slabs:]
    size = pieces[0].shape[0] - ID_ROWS
    rows = jnp.concatenate([ref[:ref.shape[0] - ID_ROWS, :] for ref in blocks], axis=0)
    ones = jnp.ones((ID_ROWS, rows.shape[0]), BF)
    row = iota((ID_ROWS, size), 0)
    for t, ref in enumerate(pieces):
        owner = me_ref[0] ^ t
        pick = one_hot(size, owner * size, ids_ref[...])
        counts = dot_nt(ones, pick).astype(jnp.int32)
        halves = jnp.where(row == 0, counts >> 5, jnp.where(row == 1, counts & 31, 0))
        ref[:size, :] = dot(pick, rows).astype(ref.dtype)
        ref[size:, :] = jnp.zeros((ID_ROWS, H), ref.dtype)
        ref[size:, :size] = halves.astype(F32).astype(ref.dtype)


def sum_prod(me, ids, blocks, size, slabs, after):
    piece = lambda kind: jax.ShapeDtypeStruct((size // slabs + ID_ROWS, H), kind)
    return pl.pallas_call(
        functools.partial(prod_sum_kernel, slabs, len(blocks)),
        in_specs=[SMEM] + [VMEM] * (1 + len(blocks)) + [ANY] * len(after),
        out_specs=[VMEM] * slabs,
        out_shape=[piece(F32)] + [piece(BF)] * (slabs - 1),
        compiler_params=PARAMS,
        name="sum_prod",
    )(me, ids, *blocks, *after)


def prod_update_kernel(slabs, me_ref, state_ref, w_ref, *rest):
    new_ref = rest[-1]
    size = new_ref.shape[0]
    first = pl.multiple_of(me_ref[0] * size, size)
    totals = sum(ref[:size, :].astype(F32) for ref in rest[:slabs])
    halves = sum(ref[size:, :size].astype(F32) for ref in rest[:slabs])
    count_row = halves[0:1, :] * 32.0 + halves[1:2, :]
    diagonal = iota((size, size), 0) == iota((size, size), 1)
    counts = jnp.sum(jnp.where(diagonal, count_row, 0.0), axis=1, keepdims=True)
    new_ref[...] = refresh(totals, counts, state_ref[pl.ds(first, size), :], w_ref[...])


def update_prod(me, state, weight, pieces, after):
    slabs = len(pieces)
    return pl.pallas_call(
        functools.partial(prod_update_kernel, slabs),
        in_specs=[SMEM] + [VMEM] * (2 + slabs) + [ANY] * len(after),
        out_specs=VMEM,
        out_shape=jax.ShapeDtypeStruct((state.shape[0] // slabs, H), BF),
        compiler_params=PARAMS,
        name="update_prod",
    )(me, state, weight, *pieces, *after)


def prod_reply_kernel(slabs, parts, me_ref, ids_ref, *rest):
    pieces, new_ref, reply_refs = rest[:slabs], rest[-1 - parts], rest[-parts:]
    size = pieces[0].shape[0]
    reply = None
    for t, ref in enumerate(pieces):
        first = pl.multiple_of((me_ref[0] ^ t) * size, size)
        new_ref[pl.ds(first, size), :] = ref[...]
        term = dot_t(one_hot(size, first, ids_ref[...]), ref[...])
        reply = term if reply is None else reply + term
    rows = reply_refs[0].shape[0]
    for s, ref in enumerate(reply_refs):
        ref[...] = reply[s * rows:(s + 1) * rows].astype(BF)


def reply_prod(me, ids, pieces, parts, after):
    slabs = len(pieces)
    size, rows = pieces[0].shape[0] * slabs, ids.shape[1]
    out = pl.pallas_call(
        functools.partial(prod_reply_kernel, slabs, parts),
        in_specs=[SMEM] + [VMEM] * (1 + slabs) + [ANY] * len(after),
        out_specs=[VMEM] * (1 + parts),
        out_shape=[jax.ShapeDtypeStruct((size, H), BF)]
        + [jax.ShapeDtypeStruct((rows // parts, H), BF)] * parts,
        compiler_params=PARAMS,
        name="reply_prod",
    )(me, ids, *pieces, *after)
    return out[0], out[1:]


def pick_rows(order, refs):
    rows = jnp.concatenate([ref[...] for ref in refs], axis=0)
    return dot_t(one_hot(rows.shape[0], 0, order), rows).astype(BF)


def finish_cust_kernel(order_ref, h_ref, w_ref, *rest):
    back = pick_rows(order_ref[0:1, :], rest[:-1])
    rest[-1][...] = h_ref[...].astype(F32) + dot(back, w_ref[:H, :])


def finish_cust(order, review_h, w_back, cust_back):
    return pl.pallas_call(
        finish_cust_kernel,
        in_specs=[VMEM] * (3 + len(cust_back)),
        out_specs=VMEM,
        out_shape=jax.ShapeDtypeStruct(review_h.shape, F32),
        compiler_params=PARAMS,
        name="finish_cust",
    )(order, review_h, w_back, *cust_back)


def finish_kernel(order_ref, part_ref, w_ref, *rest):
    back = pick_rows(order_ref[1:2, :], rest[:-1])
    rest[-1][...] = rms_norm(part_ref[...] + dot(back, w_ref[H:, :])).astype(BF)


def finish(order, part, w_back, prod_back):
    return pl.pallas_call(
        finish_kernel,
        in_specs=[VMEM] * (3 + len(prod_back)),
        out_specs=VMEM,
        out_shape=jax.ShapeDtypeStruct(part.shape, BF),
        compiler_params=PARAMS,
        name="finish",
    )(order, part, w_back, *prod_back)


def halve_kernel(parts, *refs):
    half = refs[0].shape[0] // 2
    for u, ref in enumerate(refs[-2:]):
        for s in range(parts):
            ref[s * half:(s + 1) * half, :] = refs[s][u * half:(u + 1) * half, :]


def halve(parts, after):
    rows = sum(part.shape[0] for part in parts) // 2
    return pl.pallas_call(
        functools.partial(halve_kernel, len(parts)),
        in_specs=[VMEM] * len(parts) + [ANY] * len(after),
        out_specs=[VMEM] * 2,
        out_shape=[jax.ShapeDtypeStruct((rows, H), BF)] * 2,
        compiler_params=PARAMS,
        name="halve_product_replies",
    )(*parts, *after)


def swap(value, axis, by):
    if by == 0:
        return value
    return lax.ppermute(value, axis, [(i, i ^ by) for i in range(lax.axis_size(axis))])


def rows_of(parts, start, size):
    return jnp.concatenate([part[start:start + size] for part in parts], axis=0)


def on_device(
    review_cols,
    cust_state,
    prod_state,
    w_qkv,
    w_out,
    w_msg,
    w_cust_up,
    w_prod_up,
    w_back,
    cust_slot,
    prod_slot,
    prod_pos,
    live_count,
):
    rows = review_cols.shape[0]
    nr, nz, nc = lax.axis_size("rev"), lax.axis_size("cust"), lax.axis_size("prod")
    mr, mz, mc = lax.axis_index("rev"), lax.axis_index("cust"), lax.axis_index("prod")
    cs = rows // (nr * nz)
    ps = rows // (nz * nc)
    wide = rows // nz
    me = jnp.stack([mr, mz, mc])
    flat = lambda ids: ids.reshape(1, rows)
    review_h, order, cust_blocks, prod_blocks = encode(
        (nr, nz, nc),
        me,
        review_cols,
        w_qkv,
        w_out,
        w_msg,
        flat(prod_pos),
        flat(cust_slot),
        flat(prod_slot),
        live_count,
    )

    prod_peer = swap(prod_blocks[1], "prod", 1)
    got = [swap(cust_blocks[s], "cust", s) for s in range(nz)]
    prod_blocks = pair(nz, prod_blocks[0], prod_peer, got[1:])
    prod_got = [swap(prod_blocks[s], "cust", s) for s in range(nz)]

    groups = regroup(cs, nr, got, prod_blocks[1:])
    groups = [swap(groups[t], "rev", t) for t in range(nr)]
    own = join(groups, prod_got[1:3])
    peer = swap(own, "prod", 1)

    prod_in = jnp.concatenate([ids_in(block[wide:, :wide]) for block in prod_got], axis=1)
    pieces = sum_prod(me, prod_in, prod_got, prod_state.shape[0], nr, [])
    new_cust, reply = update_cust(nr, own, peer, cust_state, w_cust_up, [])
    pieces = [swap(pieces[t], "rev", t) for t in range(nr)]
    blocks = reply.reshape(nr, nz, cs, H)
    cust_got = [swap(blocks[:, s].reshape(wide, H), "cust", s) for s in range(nz)]

    cust_back = [swap(rows_of(cust_got, t * cs, cs), "rev", t) for t in range(nr)]

    new_piece = update_prod(me, prod_state, w_prod_up, pieces, cust_got[1:3])
    new_pieces = [swap(new_piece, "rev", t) for t in range(nr)]
    new_prod, replies = reply_prod(me, prod_in, new_pieces, nz, cust_got[3:])
    replies = [swap(replies[s], "cust", s) for s in range(nz)]
    part = finish_cust(order, review_h, w_back, cust_back)
    own_replies, peer_replies = halve(replies, [part])
    prod_back = [own_replies, swap(peer_replies, "prod", 1)]

    review_out = finish(order, part, w_back, prod_back)
    return (review_out, new_cust, new_prod)


def solution(mesh):
    every = P(("rev", "cust", "prod"))
    in_specs = (
        P(("rev", "cust", "prod"), None),
        P(("rev", "cust"), None),
        P(("cust", "prod"), None),
        P(),
        P(),
        P(),
        P(),
        P(),
        P(),
        every,
        every,
        P(("rev", "cust", "prod"), None),
        P(("rev", "cust", "prod"), None),
    )
    out_specs = (
        P(("rev", "cust", "prod"), None),
        P(("rev", "cust"), None),
        P(("cust", "prod"), None),
    )
    return jax.shard_map(
        on_device, mesh=mesh, in_specs=in_specs, out_specs=out_specs, check_vma=False
    )
```

```python
import functools
import math

import jax
import jax.numpy as jnp
from jax import lax
from jax.experimental import pallas as pl
from jax.experimental.pallas import tpu as pltpu
from jax.sharding import PartitionSpec as P

H = 512
HEADS = 8
NCOL = 4
HD = 64
EPS = 1e-06
BF = jnp.bfloat16
F32 = jnp.float32
ID_ROWS = 16
LANES = 128
VMEM = pl.BlockSpec(memory_space=pltpu.VMEM)
HBM = pl.BlockSpec(memory_space=pltpu.HBM)
ANY = pl.BlockSpec(memory_space=pl.ANY)
PARAMS = pltpu.CompilerParams(vmem_limit_bytes=16 * 1024 * 1024)
ENCODE_PARAMS = pltpu.CompilerParams(vmem_limit_bytes=52 * 1024 * 1024)


def rms_norm(vector):
    return vector * lax.rsqrt(jnp.mean(vector * vector, axis=-1, keepdims=True) + EPS)


def dot(left, right):
    return jnp.dot(left, right, preferred_element_type=F32)


def dot_t(left, right):
    return lax.dot_general(left, right, (((0,), (0,)), ((), ())), preferred_element_type=F32)


def dot_nt(left, right):
    return lax.dot_general(left, right, (((1,), (1,)), ((), ())), preferred_element_type=F32)


def one_hot(rows, first, ids):
    row = lax.broadcasted_iota(jnp.int32, (rows, ids.shape[1]), 0) + first
    return jnp.where(row == ids, 1.0, 0.0).astype(BF)


def iota(shape, dim):
    return lax.broadcasted_iota(jnp.int32, shape, dim)


def encode_rows(tokens, w_qkv, w_out, pair_sum, spread, before):
    rows = tokens[0].shape[0]
    stacked = jnp.concatenate(tokens, axis=0)
    part = []
    for which in range(3):
        before(which)
        made = dot(stacked, w_qkv[:, which * H:(which + 1) * H]).astype(BF)
        part.append([made[c * rows:(c + 1) * rows] for c in range(NCOL)])
    query, key, value = part
    lane = iota((rows, 128), 1)
    scores = jnp.zeros((rows, 128), F32)
    for j in range(NCOL):
        both = dot(jnp.concatenate([query[i] * key[j] for i in range(NCOL)], axis=0), pair_sum)
        for i in range(NCOL):
            scores = jnp.where(lane >> 3 == j * NCOL + i, both[i * rows:(i + 1) * rows], scores)
    scores = scores * (1.0 / math.sqrt(HD))
    top = jnp.maximum(scores, pltpu.roll(scores, 64, 1))
    top = jnp.maximum(top, pltpu.roll(top, 32, 1))
    expon = jnp.exp(scores - top)
    total = expon + pltpu.roll(expon, 64, 1)
    total = total + pltpu.roll(total, 32, 1)
    weight = (expon / total).astype(BF).astype(F32)
    attended = jnp.zeros((rows, H), F32)
    pooled = jnp.zeros((rows, H), F32)
    for j in range(NCOL):
        turned = pltpu.roll(weight, (128 - NCOL * HEADS * j) % 128, 1).astype(BF)
        attended = attended + dot(turned, spread) * value[j].astype(F32)
        pooled = pooled + tokens[j].astype(F32)
    before(3)
    mixed = dot((attended * (1.0 / NCOL)).astype(BF), w_out[...])
    return rms_norm(pooled * (1.0 / NCOL) + mixed).astype(BF)


def halves_at(ids, place, count):
    row = iota((count, ids.shape[1]), 0)
    halves = jnp.where((row & 1) == 0, ids >> 5, ids & 31)
    return jnp.where(row >> 1 == place, halves, 0).astype(F32).astype(BF)


def id_rows(count):
    return -(-2 * count // ID_ROWS) * ID_ROWS


def split(index, size):
    if size & (size - 1) == 0:
        return index >> (size.bit_length() - 1), index & (size - 1)
    return lax.div(index, size), lax.rem(index, size)


def send_orders(sizes, index_ref):
    nr, nz, nc = sizes
    rows = index_ref.shape[1]
    cs, ps = rows // (nr * nz), rows // (nz * nc)
    mr, mz, mc = lax.axis_index("rev"), lax.axis_index("cust"), lax.axis_index("prod")
    pos, cust_slot, prod_slot = (index_ref[n:n + 1, :] for n in range(3))
    block, k = split(iota((1, rows), 1), cs)
    r, z = split(block, nz)
    counts = index_ref[3:4, :LANES].astype(F32).astype(BF)
    live = dot(counts, one_hot(LANES, 0, block)).astype(jnp.int32)
    cust = mz ^ z, mr ^ r, k, jnp.where(k < live, cust_slot + 1, 0)
    prod_id = jnp.where(k < live, prod_slot + 1, 0)
    block, k = split(pos, ps)
    z, c = split(block, nc)
    return cust, (mz ^ z, mc ^ c, k, prod_id)


def encode_kernel(sizes, rows, *refs):
    x_hbm, w_qkv_hbm, w_out_hbm, w_msg_hbm, index_ref, h_ref, order_ref = refs[:7]
    x_ref, w_qkv, w_out, w_msg, sem = refs[-5:]
    nr, nz, nc = sizes
    cust_refs, prod_refs = refs[7:7 + nz], refs[7 + nz:-5]
    chunks = x_hbm.shape[0] // rows
    copy = pltpu.make_async_copy
    x_copies = [
        copy(x_hbm.at[pl.ds(c * rows, rows)], x_ref.at[pl.ds(c * rows, rows)], sem.at[c])
        for c in range(chunks)
    ]
    w_copies = [
        copy(w_qkv_hbm.at[:, pl.ds(k * H, H)], w_qkv.at[:, pl.ds(k * H, H)], sem.at[chunks + k])
        for k in range(3)
    ]
    w_copies.append(copy(w_out_hbm, w_out, sem.at[chunks + 3]))
    last = copy(w_msg_hbm, w_msg, sem.at[chunks + 4])
    x_copies[0].start()
    w_copies[0].start()
    w_copies[1].start()
    pair_sum = jnp.where(iota((H, 128), 0) >> 6 == (iota((H, 128), 1) & 7), 1.0, 0.0).astype(BF)
    spread = jnp.where(
        (iota((128, H), 0) < NCOL * HEADS) & ((iota((128, H), 0) & 7) == iota((128, H), 1) >> 6),
        1.0,
        0.0,
    ).astype(BF)

    def first_before(which):
        w_copies[which].wait()
        if which == 0:
            w_copies[2].start()
            for x_copy in x_copies[1:]:
                x_copy.start()
        if which == 1:
            w_copies[3].start()
            last.start()

    for c in range(chunks):
        x_copies[c].wait()
        at = slice(c * rows, (c + 1) * rows)
        tokens = [x_ref[at, k * H:(k + 1) * H] for k in range(NCOL)]
        before = first_before if c == 0 else lambda which: None
        h_ref[at, :] = encode_rows(tokens, w_qkv, w_out, pair_sum, spread, before)
    (s_of, t_of, k, ids), (ps_of, u_of, pk, prod_ids) = send_orders(sizes, index_ref)
    count = h_ref.shape[0]
    cs, ps = count // (nr * nz), count // (nz * nc)
    cust_sent, prod_sent = (s_of * nr + t_of) * cs + k, (u_of * nz + ps_of) * ps + pk
    order_ref[0:1, :] = (t_of * nz + s_of) * cs + k
    order_ref[1:2, :] = prod_sent
    lanes = one_hot(nz * cs, 0, s_of * cs + k)
    halves = halves_at(ids, t_of, id_rows(nr))
    cust_ids = [
        dot_nt(jnp.where(s_of == s, halves, jnp.zeros_like(halves)), lanes) for s in range(nz)
    ]
    lanes = one_hot(nc * ps, 0, u_of * ps + pk)
    halves = halves_at(prod_ids, ps_of * (ID_ROWS // 2), nz * ID_ROWS)
    prod_ids = [
        dot_nt(jnp.where(u_of == u, halves, jnp.zeros_like(halves)), lanes) for u in range(nc)
    ]
    last.wait()
    message = dot(h_ref[...], w_msg[...]).astype(BF)
    for sent, made, refs, which in (
        (cust_sent, cust_ids, cust_refs, 0),
        (prod_sent, prod_ids, prod_refs, 1),
    ):
        size = count // len(refs)
        for s, ref in enumerate(refs):
            pick = one_hot(size, s * size, sent)
            ref[:size, :] = dot(pick, message[:, which * H:(which + 1) * H]).astype(BF)
            ref[size:, :] = jnp.zeros((ref.shape[0] - size, H), BF)
            ref[size:, :made[s].shape[1]] = made[s].astype(BF)


def encode(sizes, review_cols, w_qkv, w_out, w_msg, index):
    count = review_cols.shape[0]
    nr, nz, nc = sizes
    rows = min(count, 256)
    cust_block = jax.ShapeDtypeStruct((count // nz + id_rows(nr), H), BF)
    prod_block = jax.ShapeDtypeStruct((count // nc + nz * ID_ROWS, H), BF)
    out = pl.pallas_call(
        functools.partial(encode_kernel, sizes, rows),
        in_specs=[HBM] * 4 + [VMEM],
        out_specs=[VMEM] * (2 + nz + nc),
        out_shape=[
            jax.ShapeDtypeStruct((count, H), BF),
            jax.ShapeDtypeStruct((2, count), jnp.int32),
        ]
        + [cust_block] * nz
        + [prod_block] * nc,
        scratch_shapes=[pltpu.VMEM(a.shape, BF) for a in (review_cols, w_qkv, w_out, w_msg)]
        + [pltpu.SemaphoreType.DMA((count // rows + 5,))],
        compiler_params=ENCODE_PARAMS,
        name="encode",
    )(review_cols, w_qkv, w_out, w_msg, index)
    return out[0], out[1], out[2:2 + nz], out[2 + nz:]


def pair_kernel(parts, own_ref, peer_ref, *refs):
    part = (own_ref.shape[0] - parts * ID_ROWS) // parts
    for s, ref in enumerate(refs[-parts:]):
        at = parts * part + s * ID_ROWS
        ref[:part, :] = own_ref[s * part:(s + 1) * part, :]
        ref[part:2 * part, :] = peer_ref[s * part:(s + 1) * part, :]
        ref[2 * part:, :] = own_ref[at:at + ID_ROWS, :] + peer_ref[at:at + ID_ROWS, :]


def pair(parts, own, peer, after):
    part = (own.shape[0] - parts * ID_ROWS) // parts
    return pl.pallas_call(
        functools.partial(pair_kernel, parts),
        in_specs=[VMEM] * 2 + [ANY] * len(after),
        out_specs=[VMEM] * parts,
        out_shape=[jax.ShapeDtypeStruct((2 * part + ID_ROWS, H), BF)] * parts,
        compiler_params=PARAMS,
        name="pair_product_blocks",
    )(own, peer, *after)


def regroup_kernel(size, parts, groups, *refs):
    held = groups * size
    for t, ref in enumerate(refs[-groups:]):
        for s in range(parts):
            ref[s * size:(s + 1) * size, :] = refs[s][t * size:(t + 1) * size, :]
        if held < refs[0].shape[0]:
            ref[parts * size:, :] = sum(refs[s][held:, :] for s in range(parts))


def regroup(size, groups, got, after):
    parts, ids = len(got), got[0].shape[0] - groups * size
    if size % 16:
        tail = sum(p[groups * size:] for p in got)
        return [
            jnp.concatenate([p[t * size:(t + 1) * size] for p in got] + [tail], axis=0)
            for t in range(groups)
        ]
    return pl.pallas_call(
        functools.partial(regroup_kernel, size, parts, groups),
        in_specs=[VMEM] * parts + [ANY] * len(after),
        out_specs=[VMEM] * groups,
        out_shape=[jax.ShapeDtypeStruct((parts * size + ids, H), BF)] * groups,
        compiler_params=PARAMS,
        name="regroup_customer_blocks",
    )(*got, *after)


def join_kernel(count, *refs):
    at = 0
    for ref in refs[:count]:
        refs[-1][at:at + ref.shape[0], :] = ref[...]
        at += ref.shape[0]


def join(parts, after):
    rows = sum(part.shape[0] for part in parts)
    return pl.pallas_call(
        functools.partial(join_kernel, len(parts)),
        in_specs=[VMEM] * len(parts) + [ANY] * len(after),
        out_specs=VMEM,
        out_shape=jax.ShapeDtypeStruct((rows, H), BF),
        compiler_params=PARAMS,
        name="join",
    )(*parts, *after)


def refresh(totals, counts, states, weight):
    average = (totals / jnp.sqrt(jnp.maximum(counts, 1.0))).astype(BF)
    update = dot(average, weight)
    update = update * (1.0 / (1.0 + jnp.exp(-update)))
    return rms_norm(states.astype(F32) + update).astype(BF)


def count_of(pick):
    return jnp.sum(pick.astype(F32), axis=1, keepdims=True)


def ids_in(rows):
    rows = rows.astype(F32)
    return (rows[0:1, :] * 32.0 + rows[1:2, :]).astype(jnp.int32) - 1


def cust_kernel(groups, own_ref, peer_ref, state_ref, w_ref, *refs):
    new_ref, reply_ref = refs[-2:]
    size = state_ref.shape[0]
    held = own_ref.shape[0] // groups
    rows = held - id_rows(groups)
    totals, counts = jnp.zeros((size, H), F32), jnp.zeros((size, 1), F32)
    for ref in (peer_ref, own_ref):
        ids = [
            ids_in(ref[t * held + rows:(t + 1) * held, :rows][2 * t:2 * t + 2, :])
            for t in range(groups)
        ]
        pick = one_hot(size, 0, jnp.concatenate(ids, axis=1))
        messages = [ref[t * held:t * held + rows, :] for t in range(groups)]
        totals = totals + dot(pick, jnp.concatenate(messages, axis=0))
        counts = counts + count_of(pick)
    new = refresh(totals, counts, state_ref[...], w_ref[...])
    new_ref[...] = new
    reply_ref[...] = dot_t(pick, new).astype(BF)


def update_cust(groups, own, peer, state, weight, after):
    rows = own.shape[0] - groups * id_rows(groups)
    return pl.pallas_call(
        functools.partial(cust_kernel, groups),
        in_specs=[VMEM] * 4 + [ANY] * len(after),
        out_specs=[VMEM] * 2,
        out_shape=[
            jax.ShapeDtypeStruct(state.shape, BF),
            jax.ShapeDtypeStruct((rows, H), BF),
        ],
        compiler_params=PARAMS,
        name="update_cust",
    )(own, peer, state, weight, *after)


def prod_sum_kernel(slabs, parts, ids_ref, *refs):
    blocks, pieces = refs[:parts], refs[-slabs:]
    size = pieces[0].shape[0] - ID_ROWS
    rows = jnp.concatenate([ref[:ref.shape[0] - ID_ROWS, :] for ref in blocks], axis=0)
    ones = jnp.ones((ID_ROWS, rows.shape[0]), BF)
    row = iota((ID_ROWS, size), 0)
    for t, ref in enumerate(pieces):
        owner = lax.axis_index("rev") ^ t
        pick = one_hot(size, owner * size, ids_ref[...])
        counts = dot_nt(ones, pick).astype(jnp.int32)
        halves = jnp.where(row == 0, counts >> 5, jnp.where(row == 1, counts & 31, 0))
        ref[:size, :] = dot(pick, rows).astype(ref.dtype)
        ref[size:, :] = jnp.zeros((ID_ROWS, H), ref.dtype)
        ref[size:, :size] = halves.astype(F32).astype(ref.dtype)


def sum_prod(ids, blocks, size, slabs, after):
    piece = lambda kind: jax.ShapeDtypeStruct((size // slabs + ID_ROWS, H), kind)
    return pl.pallas_call(
        functools.partial(prod_sum_kernel, slabs, len(blocks)),
        in_specs=[VMEM] * (1 + len(blocks)) + [ANY] * len(after),
        out_specs=[VMEM] * slabs,
        out_shape=[piece(F32)] + [piece(BF)] * (slabs - 1),
        compiler_params=PARAMS,
        name="sum_prod",
    )(ids, *blocks, *after)


def prod_update_kernel(slabs, state_ref, w_ref, *rest):
    new_ref = rest[-1]
    size = new_ref.shape[0]
    first = pl.multiple_of(lax.axis_index("rev") * size, size)
    totals = sum(ref[:size, :].astype(F32) for ref in rest[:slabs])
    halves = sum(ref[size:, :size].astype(F32) for ref in rest[:slabs])
    count_row = halves[0:1, :] * 32.0 + halves[1:2, :]
    diagonal = iota((size, size), 0) == iota((size, size), 1)
    counts = jnp.sum(jnp.where(diagonal, count_row, 0.0), axis=1, keepdims=True)
    new_ref[...] = refresh(totals, counts, state_ref[pl.ds(first, size), :], w_ref[...])


def update_prod(state, weight, pieces, after):
    slabs = len(pieces)
    return pl.pallas_call(
        functools.partial(prod_update_kernel, slabs),
        in_specs=[VMEM] * (2 + slabs) + [ANY] * len(after),
        out_specs=VMEM,
        out_shape=jax.ShapeDtypeStruct((state.shape[0] // slabs, H), BF),
        compiler_params=PARAMS,
        name="update_prod",
    )(state, weight, *pieces, *after)


def prod_reply_kernel(slabs, parts, ids_ref, *rest):
    pieces, new_ref, reply_refs = rest[:slabs], rest[-1 - parts], rest[-parts:]
    size = pieces[0].shape[0]
    reply = None
    for t, ref in enumerate(pieces):
        first = pl.multiple_of((lax.axis_index("rev") ^ t) * size, size)
        new_ref[pl.ds(first, size), :] = ref[...]
        term = dot_t(one_hot(size, first, ids_ref[...]), ref[...])
        reply = term if reply is None else reply + term
    rows = reply_refs[0].shape[0]
    for s, ref in enumerate(reply_refs):
        ref[...] = reply[s * rows:(s + 1) * rows].astype(BF)


def reply_prod(ids, pieces, parts, after):
    slabs = len(pieces)
    size, rows = pieces[0].shape[0] * slabs, ids.shape[1]
    out = pl.pallas_call(
        functools.partial(prod_reply_kernel, slabs, parts),
        in_specs=[VMEM] * (1 + slabs) + [ANY] * len(after),
        out_specs=[VMEM] * (1 + parts),
        out_shape=[jax.ShapeDtypeStruct((size, H), BF)]
        + [jax.ShapeDtypeStruct((rows // parts, H), BF)] * parts,
        compiler_params=PARAMS,
        name="reply_prod",
    )(ids, *pieces, *after)
    return out[0], out[1:]


def pick_rows(order, refs):
    rows = jnp.concatenate([ref[...] for ref in refs], axis=0)
    return dot_t(one_hot(rows.shape[0], 0, order), rows).astype(BF)


def finish_cust_kernel(order_ref, h_ref, w_ref, *rest):
    back = pick_rows(order_ref[0:1, :], rest[:-1])
    rest[-1][...] = h_ref[...].astype(F32) + dot(back, w_ref[:H, :])


def finish_cust(order, review_h, w_back, cust_back):
    return pl.pallas_call(
        finish_cust_kernel,
        in_specs=[VMEM] * (3 + len(cust_back)),
        out_specs=VMEM,
        out_shape=jax.ShapeDtypeStruct(review_h.shape, F32),
        compiler_params=PARAMS,
        name="finish_cust",
    )(order, review_h, w_back, *cust_back)


def finish_kernel(order_ref, part_ref, w_ref, *rest):
    back = pick_rows(order_ref[1:2, :], rest[:-1])
    rest[-1][...] = rms_norm(part_ref[...] + dot(back, w_ref[H:, :])).astype(BF)


def finish(order, part, w_back, prod_back):
    return pl.pallas_call(
        finish_kernel,
        in_specs=[VMEM] * (3 + len(prod_back)),
        out_specs=VMEM,
        out_shape=jax.ShapeDtypeStruct(part.shape, BF),
        compiler_params=PARAMS,
        name="finish",
    )(order, part, w_back, *prod_back)


def halve_kernel(parts, *refs):
    half = refs[0].shape[0] // 2
    for u, ref in enumerate(refs[-2:]):
        for s in range(parts):
            ref[s * half:(s + 1) * half, :] = refs[s][u * half:(u + 1) * half, :]


def halve(parts, after):
    rows = sum(part.shape[0] for part in parts) // 2
    return pl.pallas_call(
        functools.partial(halve_kernel, len(parts)),
        in_specs=[VMEM] * len(parts) + [ANY] * len(after),
        out_specs=[VMEM] * 2,
        out_shape=[jax.ShapeDtypeStruct((rows, H), BF)] * 2,
        compiler_params=PARAMS,
        name="halve_product_replies",
    )(*parts, *after)


def swap(value, axis, by):
    if by == 0:
        return value
    return lax.ppermute(value, axis, [(i, i ^ by) for i in range(lax.axis_size(axis))])


def rows_of(parts, start, size):
    return jnp.concatenate([part[start:start + size] for part in parts], axis=0)


def on_device(
    review_cols,
    cust_state,
    prod_state,
    w_qkv,
    w_out,
    w_msg,
    w_cust_up,
    w_prod_up,
    w_back,
    cust_slot,
    prod_slot,
    prod_pos,
    live_count,
):
    rows = review_cols.shape[0]
    nr, nz, nc = lax.axis_size("rev"), lax.axis_size("cust"), lax.axis_size("prod")
    cs = rows // (nr * nz)
    ps = rows // (nz * nc)
    wide = rows // nz
    index = jnp.concatenate(
        [
            prod_pos,
            cust_slot.reshape(1, rows),
            prod_slot.reshape(1, rows),
            jnp.pad(live_count, ((0, 0), (0, rows - nr * nz))),
        ],
        axis=0,
    )
    review_h, order, cust_blocks, prod_blocks = encode(
        (nr, nz, nc), review_cols, w_qkv, w_out, w_msg, index
    )

    prod_peer = swap(prod_blocks[1], "prod", 1)
    got = [swap(cust_blocks[s], "cust", s) for s in range(nz)]
    prod_blocks = pair(nz, prod_blocks[0], prod_peer, got[1:])
    prod_got = [swap(prod_blocks[s], "cust", s) for s in range(nz)]

    groups = regroup(cs, nr, got, prod_blocks[1:])
    groups = [swap(groups[t], "rev", t) for t in range(nr)]
    own = join(groups, prod_got[1:3])
    peer = swap(own, "prod", 1)

    prod_in = jnp.concatenate([ids_in(block[wide:, :wide]) for block in prod_got], axis=1)
    pieces = sum_prod(prod_in, prod_got, prod_state.shape[0], nr, [])
    new_cust, reply = update_cust(nr, own, peer, cust_state, w_cust_up, [])
    pieces = [swap(pieces[t], "rev", t) for t in range(nr)]
    blocks = reply.reshape(nr, nz, cs, H)
    cust_got = [swap(blocks[:, s].reshape(wide, H), "cust", s) for s in range(nz)]

    new_piece = update_prod(prod_state, w_prod_up, pieces, cust_got[1:2])
    new_pieces = [swap(new_piece, "rev", t) for t in range(nr)]
    new_prod, made = reply_prod(prod_in, new_pieces, nz, cust_got[2:])
    replies = [swap(made[s], "cust", s) for s in range(nz)]
    cust_back = regroup(cs, nr, cust_got, made[:1])
    cust_back = [swap(cust_back[t], "rev", t) for t in range(nr)]
    part = finish_cust(order, review_h, w_back, cust_back)
    own_replies, peer_replies = halve(replies, [part])
    prod_back = [own_replies, swap(peer_replies, "prod", 1)]

    review_out = finish(order, part, w_back, prod_back)
    return (review_out, new_cust, new_prod)


def solution(mesh):
    every = P(("rev", "cust", "prod"))
    in_specs = (
        P(("rev", "cust", "prod"), None),
        P(("rev", "cust"), None),
        P(("cust", "prod"), None),
        P(),
        P(),
        P(),
        P(),
        P(),
        P(),
        every,
        every,
        P(("rev", "cust", "prod"), None),
        P(("rev", "cust", "prod"), None),
    )
    out_specs = (
        P(("rev", "cust", "prod"), None),
        P(("rev", "cust"), None),
        P(("cust", "prod"), None),
    )
    return jax.shard_map(
        on_device, mesh=mesh, in_specs=in_specs, out_specs=out_specs, check_vma=False
    )
```

```python
import functools
import math

import jax
import jax.numpy as jnp
from jax import lax
from jax.experimental import pallas as pl
from jax.experimental.pallas import tpu as pltpu
from jax.sharding import PartitionSpec as P

H = 512
HEADS = 8
NCOL = 4
HD = 64
EPS = 1e-06
BF = jnp.bfloat16
F32 = jnp.float32
ID_ROWS = 16
LANES = 128
VMEM = pl.BlockSpec(memory_space=pltpu.VMEM)
HBM = pl.BlockSpec(memory_space=pltpu.HBM)
ANY = pl.BlockSpec(memory_space=pl.ANY)
PARAMS = pltpu.CompilerParams(vmem_limit_bytes=16 * 1024 * 1024)
ENCODE_PARAMS = pltpu.CompilerParams(vmem_limit_bytes=52 * 1024 * 1024)


def rms_norm(vector):
    return vector * lax.rsqrt(jnp.mean(vector * vector, axis=-1, keepdims=True) + EPS)


def dot(left, right):
    return jnp.dot(left, right, preferred_element_type=F32)


def dot_t(left, right):
    return lax.dot_general(left, right, (((0,), (0,)), ((), ())), preferred_element_type=F32)


def dot_nt(left, right):
    return lax.dot_general(left, right, (((1,), (1,)), ((), ())), preferred_element_type=F32)


def one_hot(rows, first, ids):
    row = lax.broadcasted_iota(jnp.int32, (rows, ids.shape[1]), 0) + first
    return jnp.where(row == ids, 1.0, 0.0).astype(BF)


def iota(shape, dim):
    return lax.broadcasted_iota(jnp.int32, shape, dim)


def encode_rows(tokens, w_qkv, w_out, pair_sum, spread, before):
    rows = tokens[0].shape[0]
    stacked = jnp.concatenate(tokens, axis=0)
    part = []
    for which in range(3):
        before(which)
        made = dot(stacked, w_qkv[:, which * H:(which + 1) * H]).astype(BF)
        part.append([made[c * rows:(c + 1) * rows] for c in range(NCOL)])
    query, key, value = part
    lane = iota((rows, 128), 1)
    scores = jnp.zeros((rows, 128), F32)
    for j in range(NCOL):
        both = dot(jnp.concatenate([query[i] * key[j] for i in range(NCOL)], axis=0), pair_sum)
        for i in range(NCOL):
            scores = jnp.where(lane >> 3 == j * NCOL + i, both[i * rows:(i + 1) * rows], scores)
    scores = scores * (1.0 / math.sqrt(HD))
    top = jnp.maximum(scores, pltpu.roll(scores, 64, 1))
    top = jnp.maximum(top, pltpu.roll(top, 32, 1))
    expon = jnp.exp(scores - top)
    total = expon + pltpu.roll(expon, 64, 1)
    total = total + pltpu.roll(total, 32, 1)
    weight = (expon / total).astype(BF).astype(F32)
    attended = jnp.zeros((rows, H), F32)
    pooled = jnp.zeros((rows, H), F32)
    for j in range(NCOL):
        turned = pltpu.roll(weight, (128 - NCOL * HEADS * j) % 128, 1).astype(BF)
        attended = attended + dot(turned, spread) * value[j].astype(F32)
        pooled = pooled + tokens[j].astype(F32)
    before(3)
    mixed = dot((attended * (1.0 / NCOL)).astype(BF), w_out[...])
    return rms_norm(pooled * (1.0 / NCOL) + mixed).astype(BF)


def halves_at(ids, place, count):
    row = iota((count, ids.shape[1]), 0)
    halves = jnp.where((row & 1) == 0, ids >> 5, ids & 31)
    return jnp.where(row >> 1 == place, halves, 0).astype(F32).astype(BF)


def id_rows(count):
    return -(-2 * count // ID_ROWS) * ID_ROWS


def split(index, size):
    if size & (size - 1) == 0:
        return index >> (size.bit_length() - 1), index & (size - 1)
    return lax.div(index, size), lax.rem(index, size)


def send_orders(sizes, index_ref):
    nr, nz, nc = sizes
    rows = index_ref.shape[1]
    cs, ps = rows // (nr * nz), rows // (nz * nc)
    mr, mz, mc = lax.axis_index("rev"), lax.axis_index("cust"), lax.axis_index("prod")
    pos, cust_slot, prod_slot = (index_ref[n:n + 1, :] for n in range(3))
    block, k = split(iota((1, rows), 1), cs)
    r, z = split(block, nz)
    counts = index_ref[3:4, :LANES].astype(F32).astype(BF)
    live = dot(counts, one_hot(LANES, 0, block)).astype(jnp.int32)
    cust = mz ^ z, mr ^ r, k, jnp.where(k < live, cust_slot + 1, 0)
    prod_id = jnp.where(k < live, prod_slot + 1, 0)
    block, k = split(pos, ps)
    z, c = split(block, nc)
    return cust, (mz ^ z, mc ^ c, k, prod_id)


def encode_kernel(sizes, rows, *refs):
    x_hbm, w_qkv_hbm, w_out_hbm, w_msg_hbm, index_ref, h_ref, order_ref = refs[:7]
    x_ref, w_qkv, w_out, w_msg, sem = refs[-5:]
    nr, nz, nc = sizes
    cust_refs, prod_refs = refs[7:7 + nz], refs[7 + nz:-5]
    chunks = x_hbm.shape[0] // rows
    copy = pltpu.make_async_copy
    x_copies = [
        copy(x_hbm.at[pl.ds(c * rows, rows)], x_ref.at[pl.ds(c * rows, rows)], sem.at[c])
        for c in range(chunks)
    ]
    w_copies = [
        copy(w_qkv_hbm.at[:, pl.ds(k * H, H)], w_qkv.at[:, pl.ds(k * H, H)], sem.at[chunks + k])
        for k in range(3)
    ]
    w_copies.append(copy(w_out_hbm, w_out, sem.at[chunks + 3]))
    last = copy(w_msg_hbm, w_msg, sem.at[chunks + 4])
    x_copies[0].start()
    w_copies[0].start()
    w_copies[1].start()
    pair_sum = jnp.where(iota((H, 128), 0) >> 6 == (iota((H, 128), 1) & 7), 1.0, 0.0).astype(BF)
    spread = jnp.where(
        (iota((128, H), 0) < NCOL * HEADS) & ((iota((128, H), 0) & 7) == iota((128, H), 1) >> 6),
        1.0,
        0.0,
    ).astype(BF)

    def first_before(which):
        w_copies[which].wait()
        if which == 0:
            w_copies[2].start()
            for x_copy in x_copies[1:]:
                x_copy.start()
        if which == 1:
            w_copies[3].start()
            last.start()

    for c in range(chunks):
        x_copies[c].wait()
        at = slice(c * rows, (c + 1) * rows)
        tokens = [x_ref[at, k * H:(k + 1) * H] for k in range(NCOL)]
        before = first_before if c == 0 else lambda which: None
        h_ref[at, :] = encode_rows(tokens, w_qkv, w_out, pair_sum, spread, before)
    (s_of, t_of, k, ids), (ps_of, u_of, pk, prod_ids) = send_orders(sizes, index_ref)
    count = h_ref.shape[0]
    cs, ps = count // (nr * nz), count // (nz * nc)
    cust_sent, prod_sent = (s_of * nr + t_of) * cs + k, (u_of * nz + ps_of) * ps + pk
    order_ref[0:1, :] = (t_of * nz + s_of) * cs + k
    order_ref[1:2, :] = prod_sent
    lanes = one_hot(nz * cs, 0, s_of * cs + k)
    halves = halves_at(ids, t_of, id_rows(nr))
    cust_ids = [
        dot_nt(jnp.where(s_of == s, halves, jnp.zeros_like(halves)), lanes) for s in range(nz)
    ]
    lanes = one_hot(nc * ps, 0, u_of * ps + pk)
    halves = halves_at(prod_ids, ps_of * (ID_ROWS // 2), nz * ID_ROWS)
    prod_ids = [
        dot_nt(jnp.where(u_of == u, halves, jnp.zeros_like(halves)), lanes) for u in range(nc)
    ]
    last.wait()
    message = dot(h_ref[...], w_msg[...]).astype(BF)
    for sent, made, refs, which in (
        (cust_sent, cust_ids, cust_refs, 0),
        (prod_sent, prod_ids, prod_refs, 1),
    ):
        size = count // len(refs)
        for s, ref in enumerate(refs):
            pick = one_hot(size, s * size, sent)
            ref[:size, :] = dot(pick, message[:, which * H:(which + 1) * H]).astype(BF)
            ref[size:, :] = jnp.zeros((ref.shape[0] - size, H), BF)
            ref[size:, :made[s].shape[1]] = made[s].astype(BF)


def encode(sizes, review_cols, w_qkv, w_out, w_msg, index):
    count = review_cols.shape[0]
    nr, nz, nc = sizes
    rows = min(count, 256)
    cust_block = jax.ShapeDtypeStruct((count // nz + id_rows(nr), H), BF)
    prod_block = jax.ShapeDtypeStruct((count // nc + nz * ID_ROWS, H), BF)
    out = pl.pallas_call(
        functools.partial(encode_kernel, sizes, rows),
        in_specs=[HBM] * 4 + [VMEM],
        out_specs=[VMEM] * (2 + nz + nc),
        out_shape=[
            jax.ShapeDtypeStruct((count, H), BF),
            jax.ShapeDtypeStruct((2, count), jnp.int32),
        ]
        + [cust_block] * nz
        + [prod_block] * nc,
        scratch_shapes=[pltpu.VMEM(a.shape, BF) for a in (review_cols, w_qkv, w_out, w_msg)]
        + [pltpu.SemaphoreType.DMA((count // rows + 5,))],
        compiler_params=ENCODE_PARAMS,
        name="encode",
    )(review_cols, w_qkv, w_out, w_msg, index)
    return out[0], out[1], out[2:2 + nz], out[2 + nz:]


def pair_kernel(parts, own_ref, peer_ref, *refs):
    part = (own_ref.shape[0] - parts * ID_ROWS) // parts
    for s, ref in enumerate(refs[-parts:]):
        at = parts * part + s * ID_ROWS
        ref[:part, :] = own_ref[s * part:(s + 1) * part, :]
        ref[part:2 * part, :] = peer_ref[s * part:(s + 1) * part, :]
        ref[2 * part:, :] = own_ref[at:at + ID_ROWS, :] + peer_ref[at:at + ID_ROWS, :]


def pair(parts, own, peer, after):
    part = (own.shape[0] - parts * ID_ROWS) // parts
    return pl.pallas_call(
        functools.partial(pair_kernel, parts),
        in_specs=[VMEM] * 2 + [ANY] * len(after),
        out_specs=[VMEM] * parts,
        out_shape=[jax.ShapeDtypeStruct((2 * part + ID_ROWS, H), BF)] * parts,
        compiler_params=PARAMS,
        name="pair_product_blocks",
    )(own, peer, *after)


def regroup_kernel(size, parts, groups, *refs):
    held = groups * size
    for t, ref in enumerate(refs[-groups:]):
        for s in range(parts):
            ref[s * size:(s + 1) * size, :] = refs[s][t * size:(t + 1) * size, :]
        if held < refs[0].shape[0]:
            ref[parts * size:, :] = sum(refs[s][held:, :] for s in range(parts))


def regroup(size, groups, got, after):
    parts, ids = len(got), got[0].shape[0] - groups * size
    if size % 16:
        tail = sum(p[groups * size:] for p in got)
        return [
            jnp.concatenate([p[t * size:(t + 1) * size] for p in got] + [tail], axis=0)
            for t in range(groups)
        ]
    return pl.pallas_call(
        functools.partial(regroup_kernel, size, parts, groups),
        in_specs=[VMEM] * parts + [ANY] * len(after),
        out_specs=[VMEM] * groups,
        out_shape=[jax.ShapeDtypeStruct((parts * size + ids, H), BF)] * groups,
        compiler_params=PARAMS,
        name="regroup_customer_blocks",
    )(*got, *after)


def join_kernel(count, *refs):
    at = 0
    for ref in refs[:count]:
        refs[-1][at:at + ref.shape[0], :] = ref[...]
        at += ref.shape[0]


def join(parts, after):
    rows = sum(part.shape[0] for part in parts)
    return pl.pallas_call(
        functools.partial(join_kernel, len(parts)),
        in_specs=[VMEM] * len(parts) + [ANY] * len(after),
        out_specs=VMEM,
        out_shape=jax.ShapeDtypeStruct((rows, H), BF),
        compiler_params=PARAMS,
        name="join",
    )(*parts, *after)


def refresh(totals, counts, states, weight):
    average = (totals / jnp.sqrt(jnp.maximum(counts, 1.0))).astype(BF)
    update = dot(average, weight)
    update = update * (1.0 / (1.0 + jnp.exp(-update)))
    return rms_norm(states.astype(F32) + update).astype(BF)


def count_of(pick):
    return jnp.sum(pick.astype(F32), axis=1, keepdims=True)


def ids_in(rows):
    rows = rows.astype(F32)
    return (rows[0:1, :] * 32.0 + rows[1:2, :]).astype(jnp.int32) - 1


def cust_kernel(groups, own_ref, peer_ref, state_ref, w_ref, *refs):
    new_ref, reply_ref = refs[-2:]
    size = state_ref.shape[0]
    held = own_ref.shape[0] // groups
    rows = held - id_rows(groups)
    totals, counts = jnp.zeros((size, H), F32), jnp.zeros((size, 1), F32)
    for ref in (peer_ref, own_ref):
        ids = [
            ids_in(ref[t * held + rows:(t + 1) * held, :rows][2 * t:2 * t + 2, :])
            for t in range(groups)
        ]
        pick = one_hot(size, 0, jnp.concatenate(ids, axis=1))
        messages = [ref[t * held:t * held + rows, :] for t in range(groups)]
        totals = totals + dot(pick, jnp.concatenate(messages, axis=0))
        counts = counts + count_of(pick)
    new = refresh(totals, counts, state_ref[...], w_ref[...])
    new_ref[...] = new
    reply_ref[...] = dot_t(pick, new).astype(BF)


def update_cust(groups, own, peer, state, weight, after):
    rows = own.shape[0] - groups * id_rows(groups)
    return pl.pallas_call(
        functools.partial(cust_kernel, groups),
        in_specs=[VMEM] * 4 + [ANY] * len(after),
        out_specs=[VMEM] * 2,
        out_shape=[
            jax.ShapeDtypeStruct(state.shape, BF),
            jax.ShapeDtypeStruct((rows, H), BF),
        ],
        compiler_params=PARAMS,
        name="update_cust",
    )(own, peer, state, weight, *after)


def prod_sum_kernel(slabs, parts, ids_ref, *refs):
    blocks, pieces = refs[:parts], refs[-slabs:]
    size = pieces[0].shape[0] - ID_ROWS
    rows = jnp.concatenate([ref[:ref.shape[0] - ID_ROWS, :] for ref in blocks], axis=0)
    ones = jnp.ones((ID_ROWS, rows.shape[0]), BF)
    row = iota((ID_ROWS, size), 0)
    for t, ref in enumerate(pieces):
        owner = lax.axis_index("rev") ^ t
        pick = one_hot(size, owner * size, ids_ref[...])
        counts = dot_nt(ones, pick).astype(jnp.int32)
        halves = jnp.where(row == 0, counts >> 5, jnp.where(row == 1, counts & 31, 0))
        ref[:size, :] = dot(pick, rows).astype(ref.dtype)
        ref[size:, :] = jnp.zeros((ID_ROWS, H), ref.dtype)
        ref[size:, :size] = halves.astype(F32).astype(ref.dtype)


def sum_prod(ids, blocks, size, slabs, after):
    piece = lambda kind: jax.ShapeDtypeStruct((size // slabs + ID_ROWS, H), kind)
    return pl.pallas_call(
        functools.partial(prod_sum_kernel, slabs, len(blocks)),
        in_specs=[VMEM] * (1 + len(blocks)) + [ANY] * len(after),
        out_specs=[VMEM] * slabs,
        out_shape=[piece(F32)] + [piece(BF)] * (slabs - 1),
        compiler_params=PARAMS,
        name="sum_prod",
    )(ids, *blocks, *after)


def prod_update_kernel(slabs, state_ref, w_ref, *rest):
    new_ref = rest[-1]
    size = new_ref.shape[0]
    first = pl.multiple_of(lax.axis_index("rev") * size, size)
    totals = sum(ref[:size, :].astype(F32) for ref in rest[:slabs])
    halves = sum(ref[size:, :size].astype(F32) for ref in rest[:slabs])
    count_row = halves[0:1, :] * 32.0 + halves[1:2, :]
    diagonal = iota((size, size), 0) == iota((size, size), 1)
    counts = jnp.sum(jnp.where(diagonal, count_row, 0.0), axis=1, keepdims=True)
    new_ref[...] = refresh(totals, counts, state_ref[pl.ds(first, size), :], w_ref[...])


def update_prod(state, weight, pieces, after):
    slabs = len(pieces)
    return pl.pallas_call(
        functools.partial(prod_update_kernel, slabs),
        in_specs=[VMEM] * (2 + slabs) + [ANY] * len(after),
        out_specs=VMEM,
        out_shape=jax.ShapeDtypeStruct((state.shape[0] // slabs, H), BF),
        compiler_params=PARAMS,
        name="update_prod",
    )(state, weight, *pieces, *after)


def prod_reply_kernel(slabs, parts, pick_ref, *rest):
    pieces, new_ref, reply_refs = rest[:slabs], rest[-1 - parts], rest[-parts:]
    size = pieces[0].shape[0]
    for t, ref in enumerate(pieces):
        first = pl.multiple_of((lax.axis_index("rev") ^ t) * size, size)
        new_ref[pl.ds(first, size), :] = ref[...]
    rows = reply_refs[0].shape[0]
    for s, ref in enumerate(reply_refs):
        ref[...] = dot(pick_ref[s * rows:(s + 1) * rows, :], new_ref[...]).astype(BF)


def reply_prod(pick, pieces, parts, after):
    slabs = len(pieces)
    size, rows = pieces[0].shape[0] * slabs, pick.shape[0]
    out = pl.pallas_call(
        functools.partial(prod_reply_kernel, slabs, parts),
        in_specs=[VMEM] * (1 + slabs) + [ANY] * len(after),
        out_specs=[VMEM] * (1 + parts),
        out_shape=[jax.ShapeDtypeStruct((size, H), BF)]
        + [jax.ShapeDtypeStruct((rows // parts, H), BF)] * parts,
        compiler_params=PARAMS,
        name="reply_prod",
    )(pick, *pieces, *after)
    return out[0], out[1:]


def turned_kernel(ids_ref, *refs):
    for n, ref in enumerate(refs):
        rows = iota((ref.shape[1], ref.shape[0]), 0)
        ref[...] = jnp.where(rows == ids_ref[n:n + 1, :], 1.0, 0.0).T.astype(BF)


def turned_picks(ids, size):
    pick = jax.ShapeDtypeStruct((ids.shape[1], size), BF)
    return pl.pallas_call(
        turned_kernel,
        in_specs=[VMEM],
        out_specs=[VMEM] * ids.shape[0],
        out_shape=[pick] * ids.shape[0],
        compiler_params=PARAMS,
        name="turned_picks",
    )(ids)


def finish_part_kernel(start, pick_ref, sum_ref, w_ref, *rest):
    rows = jnp.concatenate([ref[...] for ref in rest[:-1]], axis=0)
    at, wide = start
    back = dot(pick_ref[:, at:at + rows.shape[0]], rows).astype(BF)
    total = sum_ref[...].astype(F32) + dot(back, w_ref[wide:wide + H, :])
    if rest[-1].dtype == BF:
        total = rms_norm(total)
    rest[-1][...] = total.astype(rest[-1].dtype)


def finish_part(start, picks, total, w_back, rows, kind, name):
    return pl.pallas_call(
        functools.partial(finish_part_kernel, start),
        in_specs=[VMEM] * (3 + len(rows)),
        out_specs=VMEM,
        out_shape=jax.ShapeDtypeStruct(total.shape, kind),
        compiler_params=PARAMS,
        name=name,
    )(picks, total, w_back, *rows)


def halve_kernel(parts, *refs):
    half = refs[0].shape[0] // 2
    for u, ref in enumerate(refs[-2:]):
        for s in range(parts):
            ref[s * half:(s + 1) * half, :] = refs[s][u * half:(u + 1) * half, :]


def halve(parts, after):
    rows = sum(part.shape[0] for part in parts) // 2
    return pl.pallas_call(
        functools.partial(halve_kernel, len(parts)),
        in_specs=[VMEM] * len(parts) + [ANY] * len(after),
        out_specs=[VMEM] * 2,
        out_shape=[jax.ShapeDtypeStruct((rows, H), BF)] * 2,
        compiler_params=PARAMS,
        name="halve_product_replies",
    )(*parts, *after)


def swap(value, axis, by):
    if by == 0:
        return value
    return lax.ppermute(value, axis, [(i, i ^ by) for i in range(lax.axis_size(axis))])


def rows_of(parts, start, size):
    return jnp.concatenate([part[start:start + size] for part in parts], axis=0)


def on_device(
    review_cols,
    cust_state,
    prod_state,
    w_qkv,
    w_out,
    w_msg,
    w_cust_up,
    w_prod_up,
    w_back,
    cust_slot,
    prod_slot,
    prod_pos,
    live_count,
):
    rows = review_cols.shape[0]
    nr, nz, nc = lax.axis_size("rev"), lax.axis_size("cust"), lax.axis_size("prod")
    cs = rows // (nr * nz)
    ps = rows // (nz * nc)
    wide = rows // nz
    index = jnp.concatenate(
        [
            prod_pos,
            cust_slot.reshape(1, rows),
            prod_slot.reshape(1, rows),
            jnp.pad(live_count, ((0, 0), (0, rows - nr * nz))),
        ],
        axis=0,
    )
    review_h, order, cust_blocks, prod_blocks = encode(
        (nr, nz, nc), review_cols, w_qkv, w_out, w_msg, index
    )

    cust_pick, prod_pick = turned_picks(order, rows)

    prod_peer = swap(prod_blocks[1], "prod", 1)
    got = [swap(cust_blocks[s], "cust", s) for s in range(nz)]
    prod_blocks = pair(nz, prod_blocks[0], prod_peer, got[1:3])
    prod_got = [swap(prod_blocks[s], "cust", s) for s in range(nz)]

    groups = regroup(cs, nr, got, prod_blocks[1:])
    groups = [swap(groups[t], "rev", t) for t in range(nr)]
    own = join(groups, prod_got[1:3])
    peer = swap(own, "prod", 1)

    prod_in = jnp.concatenate([ids_in(block[wide:, :wide]) for block in prod_got], axis=1)
    pieces = sum_prod(prod_in, prod_got, prod_state.shape[0], nr, [])
    new_cust, reply = update_cust(nr, own, peer, cust_state, w_cust_up, [])
    pieces = [swap(pieces[t], "rev", t) for t in range(nr)]
    blocks = reply.reshape(nr, nz, cs, H)
    cust_got = [swap(blocks[:, s].reshape(wide, H), "cust", s) for s in range(nz)]

    new_piece = update_prod(prod_state, w_prod_up, pieces, cust_got[1:2])
    new_pieces = [swap(new_piece, "rev", t) for t in range(nr)]
    new_prod, made = reply_prod(turned_picks(prod_in, prod_state.shape[0])[0], new_pieces, nz, cust_got[2:])
    replies = [swap(made[s], "cust", s) for s in range(nz)]
    cust_back = regroup(cs, nr, cust_got, made[:1])
    cust_back = [swap(cust_back[t], "rev", t) for t in range(nr)]
    part = finish_part((0, 0), cust_pick, review_h, w_back, cust_back, F32, "finish_cust")
    own_replies, peer_replies = halve(replies, [part])
    peer_replies = swap(peer_replies, "prod", 1)
    part = finish_part((0, H), prod_pick, part, w_back, [own_replies], F32, "finish_own")
    review_out = finish_part((rows // nc, H), prod_pick, part, w_back, [peer_replies], BF, "finish")
    return (review_out, new_cust, new_prod)


def solution(mesh):
    every = P(("rev", "cust", "prod"))
    in_specs = (
        P(("rev", "cust", "prod"), None),
        P(("rev", "cust"), None),
        P(("cust", "prod"), None),
        P(),
        P(),
        P(),
        P(),
        P(),
        P(),
        every,
        every,
        P(("rev", "cust", "prod"), None),
        P(("rev", "cust", "prod"), None),
    )
    out_specs = (
        P(("rev", "cust", "prod"), None),
        P(("rev", "cust"), None),
        P(("cust", "prod"), None),
    )
    return jax.shard_map(
        on_device, mesh=mesh, in_specs=in_specs, out_specs=out_specs, check_vma=False
    )
```

```python
import functools
import math

import jax
import jax.numpy as jnp
from jax import lax
from jax.experimental import pallas as pl
from jax.experimental.pallas import tpu as pltpu
from jax.sharding import PartitionSpec as P

H = 512
HEADS = 8
NCOL = 4
HD = 64
EPS = 1e-06
BF = jnp.bfloat16
F32 = jnp.float32
ID_ROWS = 16
LANES = 128
VMEM = pl.BlockSpec(memory_space=pltpu.VMEM)
HBM = pl.BlockSpec(memory_space=pltpu.HBM)
ANY = pl.BlockSpec(memory_space=pl.ANY)
PARAMS = pltpu.CompilerParams(vmem_limit_bytes=16 * 1024 * 1024)
ENCODE_PARAMS = pltpu.CompilerParams(vmem_limit_bytes=52 * 1024 * 1024)


def rms_norm(vector):
    return vector * lax.rsqrt(jnp.mean(vector * vector, axis=-1, keepdims=True) + EPS)


def dot(left, right):
    return jnp.dot(left, right, preferred_element_type=F32)


def dot_t(left, right):
    return lax.dot_general(left, right, (((0,), (0,)), ((), ())), preferred_element_type=F32)


def dot_nt(left, right):
    return lax.dot_general(left, right, (((1,), (1,)), ((), ())), preferred_element_type=F32)


def one_hot(rows, first, ids):
    row = lax.broadcasted_iota(jnp.int32, (rows, ids.shape[1]), 0) + first
    return jnp.where(row == ids, 1.0, 0.0).astype(BF)


def iota(shape, dim):
    return lax.broadcasted_iota(jnp.int32, shape, dim)


def encode_rows(tokens, w_qkv, w_out, pair_sum, spread, before):
    rows = tokens[0].shape[0]
    stacked = jnp.concatenate(tokens, axis=0)
    part = []
    for which in range(3):
        before(which)
        made = dot(stacked, w_qkv[:, which * H:(which + 1) * H]).astype(BF)
        part.append([made[c * rows:(c + 1) * rows] for c in range(NCOL)])
    query, key, value = part
    lane = iota((rows, 128), 1)
    scores = jnp.zeros((rows, 128), F32)
    for j in range(NCOL):
        both = dot(jnp.concatenate([query[i] * key[j] for i in range(NCOL)], axis=0), pair_sum)
        for i in range(NCOL):
            scores = jnp.where(lane >> 3 == j * NCOL + i, both[i * rows:(i + 1) * rows], scores)
    scores = scores * (1.0 / math.sqrt(HD))
    top = jnp.maximum(scores, pltpu.roll(scores, 64, 1))
    top = jnp.maximum(top, pltpu.roll(top, 32, 1))
    expon = jnp.exp(scores - top)
    total = expon + pltpu.roll(expon, 64, 1)
    total = total + pltpu.roll(total, 32, 1)
    weight = (expon / total).astype(BF).astype(F32)
    attended = jnp.zeros((rows, H), F32)
    pooled = jnp.zeros((rows, H), F32)
    for j in range(NCOL):
        turned = pltpu.roll(weight, (128 - NCOL * HEADS * j) % 128, 1).astype(BF)
        attended = attended + dot(turned, spread) * value[j].astype(F32)
        pooled = pooled + tokens[j].astype(F32)
    before(3)
    mixed = dot((attended * (1.0 / NCOL)).astype(BF), w_out[...])
    return rms_norm(pooled * (1.0 / NCOL) + mixed).astype(BF)


def halves_at(ids, place, count):
    row = iota((count, ids.shape[1]), 0)
    halves = jnp.where((row & 1) == 0, ids >> 5, ids & 31)
    return jnp.where(row >> 1 == place, halves, 0).astype(F32).astype(BF)


def id_rows(count):
    return -(-2 * count // ID_ROWS) * ID_ROWS


def split(index, size):
    if size & (size - 1) == 0:
        return index >> (size.bit_length() - 1), index & (size - 1)
    return lax.div(index, size), lax.rem(index, size)


def send_orders(sizes, index_ref):
    nr, nz, nc = sizes
    rows = index_ref.shape[1]
    cs, ps = rows // (nr * nz), rows // (nz * nc)
    mr, mz, mc = lax.axis_index("rev"), lax.axis_index("cust"), lax.axis_index("prod")
    pos, cust_slot, prod_slot = (index_ref[n:n + 1, :] for n in range(3))
    block, k = split(iota((1, rows), 1), cs)
    r, z = split(block, nz)
    counts = index_ref[3:4, :LANES].astype(F32).astype(BF)
    live = dot(counts, one_hot(LANES, 0, block)).astype(jnp.int32)
    cust = mz ^ z, mr ^ r, k, jnp.where(k < live, cust_slot + 1, 0)
    prod_id = jnp.where(k < live, prod_slot + 1, 0)
    block, k = split(pos, ps)
    z, c = split(block, nc)
    return cust, (mz ^ z, mc ^ c, k, prod_id)


def encode_kernel(sizes, rows, *refs):
    x_hbm, w_qkv_hbm, w_out_hbm, w_msg_hbm, index_ref, h_ref, order_ref = refs[:7]
    x_ref, w_qkv, w_out, w_msg, sem = refs[-5:]
    nr, nz, nc = sizes
    cust_refs, prod_refs = refs[7:7 + nz], refs[7 + nz:-5]
    chunks = x_hbm.shape[0] // rows
    copy = pltpu.make_async_copy
    x_copies = [
        copy(x_hbm.at[pl.ds(c * rows, rows)], x_ref.at[pl.ds(c * rows, rows)], sem.at[c])
        for c in range(chunks)
    ]
    w_copies = [
        copy(w_qkv_hbm.at[:, pl.ds(k * H, H)], w_qkv.at[:, pl.ds(k * H, H)], sem.at[chunks + k])
        for k in range(3)
    ]
    w_copies.append(copy(w_out_hbm, w_out, sem.at[chunks + 3]))
    last = copy(w_msg_hbm, w_msg, sem.at[chunks + 4])
    x_copies[0].start()
    w_copies[0].start()
    w_copies[1].start()
    pair_sum = jnp.where(iota((H, 128), 0) >> 6 == (iota((H, 128), 1) & 7), 1.0, 0.0).astype(BF)
    spread = jnp.where(
        (iota((128, H), 0) < NCOL * HEADS) & ((iota((128, H), 0) & 7) == iota((128, H), 1) >> 6),
        1.0,
        0.0,
    ).astype(BF)

    def first_before(which):
        w_copies[which].wait()
        if which == 0:
            w_copies[2].start()
            for x_copy in x_copies[1:]:
                x_copy.start()
        if which == 1:
            w_copies[3].start()
            last.start()

    for c in range(chunks):
        x_copies[c].wait()
        at = slice(c * rows, (c + 1) * rows)
        tokens = [x_ref[at, k * H:(k + 1) * H] for k in range(NCOL)]
        before = first_before if c == 0 else lambda which: None
        h_ref[at, :] = encode_rows(tokens, w_qkv, w_out, pair_sum, spread, before)
    (s_of, t_of, k, ids), (ps_of, u_of, pk, prod_ids) = send_orders(sizes, index_ref)
    count = h_ref.shape[0]
    cs, ps = count // (nr * nz), count // (nz * nc)
    cust_sent, prod_sent = (s_of * nr + t_of) * cs + k, (u_of * nz + ps_of) * ps + pk
    order_ref[0:1, :] = (t_of * nz + s_of) * cs + k
    order_ref[1:2, :] = prod_sent
    lanes = one_hot(nz * cs, 0, s_of * cs + k)
    halves = halves_at(ids, t_of, id_rows(nr))
    cust_ids = [
        dot_nt(jnp.where(s_of == s, halves, jnp.zeros_like(halves)), lanes) for s in range(nz)
    ]
    lanes = one_hot(nc * ps, 0, u_of * ps + pk)
    halves = halves_at(prod_ids, ps_of * (ID_ROWS // 2), nz * ID_ROWS)
    prod_ids = [
        dot_nt(jnp.where(u_of == u, halves, jnp.zeros_like(halves)), lanes) for u in range(nc)
    ]
    last.wait()
    message = dot(h_ref[...], w_msg[...]).astype(BF)
    for sent, made, refs, which in (
        (cust_sent, cust_ids, cust_refs, 0),
        (prod_sent, prod_ids, prod_refs, 1),
    ):
        size = count // len(refs)
        for s, ref in enumerate(refs):
            pick = one_hot(size, s * size, sent)
            ref[:size, :] = dot(pick, message[:, which * H:(which + 1) * H]).astype(BF)
            ref[size:, :] = jnp.zeros((ref.shape[0] - size, H), BF)
            ref[size:, :made[s].shape[1]] = made[s].astype(BF)


def encode(sizes, review_cols, w_qkv, w_out, w_msg, index):
    count = review_cols.shape[0]
    nr, nz, nc = sizes
    rows = min(count, 256)
    cust_block = jax.ShapeDtypeStruct((count // nz + id_rows(nr), H), BF)
    prod_block = jax.ShapeDtypeStruct((count // nc + nz * ID_ROWS, H), BF)
    out = pl.pallas_call(
        functools.partial(encode_kernel, sizes, rows),
        in_specs=[HBM] * 4 + [VMEM],
        out_specs=[VMEM] * (2 + nz + nc),
        out_shape=[
            jax.ShapeDtypeStruct((count, H), BF),
            jax.ShapeDtypeStruct((2, count), jnp.int32),
        ]
        + [cust_block] * nz
        + [prod_block] * nc,
        scratch_shapes=[pltpu.VMEM(a.shape, BF) for a in (review_cols, w_qkv, w_out, w_msg)]
        + [pltpu.SemaphoreType.DMA((count // rows + 5,))],
        compiler_params=ENCODE_PARAMS,
        name="encode",
    )(review_cols, w_qkv, w_out, w_msg, index)
    return out[0], out[1], out[2:2 + nz], out[2 + nz:]


def pair_kernel(parts, own_ref, peer_ref, *refs):
    part = (own_ref.shape[0] - parts * ID_ROWS) // parts
    for s, ref in enumerate(refs[-parts:]):
        at = parts * part + s * ID_ROWS
        ref[:part, :] = own_ref[s * part:(s + 1) * part, :]
        ref[part:2 * part, :] = peer_ref[s * part:(s + 1) * part, :]
        ref[2 * part:, :] = own_ref[at:at + ID_ROWS, :] + peer_ref[at:at + ID_ROWS, :]


def pair(parts, own, peer, after):
    part = (own.shape[0] - parts * ID_ROWS) // parts
    return pl.pallas_call(
        functools.partial(pair_kernel, parts),
        in_specs=[VMEM] * 2 + [ANY] * len(after),
        out_specs=[VMEM] * parts,
        out_shape=[jax.ShapeDtypeStruct((2 * part + ID_ROWS, H), BF)] * parts,
        compiler_params=PARAMS,
        name="pair_product_blocks",
    )(own, peer, *after)


def regroup_kernel(size, parts, groups, *refs):
    held = groups * size
    for t, ref in enumerate(refs[-groups:]):
        for s in range(parts):
            ref[s * size:(s + 1) * size, :] = refs[s][t * size:(t + 1) * size, :]
        if held < refs[0].shape[0]:
            ref[parts * size:, :] = sum(refs[s][held:, :] for s in range(parts))


def regroup(size, groups, got, after):
    parts, ids = len(got), got[0].shape[0] - groups * size
    if size % 16:
        tail = sum(p[groups * size:] for p in got)
        return [
            jnp.concatenate([p[t * size:(t + 1) * size] for p in got] + [tail], axis=0)
            for t in range(groups)
        ]
    return pl.pallas_call(
        functools.partial(regroup_kernel, size, parts, groups),
        in_specs=[VMEM] * parts + [ANY] * len(after),
        out_specs=[VMEM] * groups,
        out_shape=[jax.ShapeDtypeStruct((parts * size + ids, H), BF)] * groups,
        compiler_params=PARAMS,
        name="regroup_customer_blocks",
    )(*got, *after)


def join_kernel(count, *refs):
    at = 0
    for ref in refs[:count]:
        refs[-1][at:at + ref.shape[0], :] = ref[...]
        at += ref.shape[0]


def join(parts, after):
    rows = sum(part.shape[0] for part in parts)
    return pl.pallas_call(
        functools.partial(join_kernel, len(parts)),
        in_specs=[VMEM] * len(parts) + [ANY] * len(after),
        out_specs=VMEM,
        out_shape=jax.ShapeDtypeStruct((rows, H), BF),
        compiler_params=PARAMS,
        name="join",
    )(*parts, *after)


def refresh(totals, counts, states, weight):
    average = (totals / jnp.sqrt(jnp.maximum(counts, 1.0))).astype(BF)
    update = dot(average, weight)
    update = update * (1.0 / (1.0 + jnp.exp(-update)))
    return rms_norm(states.astype(F32) + update).astype(BF)


def count_of(pick):
    return jnp.sum(pick.astype(F32), axis=1, keepdims=True)


def ids_in(rows):
    rows = rows.astype(F32)
    return (rows[0:1, :] * 32.0 + rows[1:2, :]).astype(jnp.int32) - 1


def cust_kernel(groups, own_ref, peer_ref, state_ref, w_ref, *refs):
    new_ref, reply_ref = refs[-2:]
    size = state_ref.shape[0]
    held = own_ref.shape[0] // groups
    rows = held - id_rows(groups)
    totals, counts = jnp.zeros((size, H), F32), jnp.zeros((size, 1), F32)
    for ref in (peer_ref, own_ref):
        ids = [
            ids_in(ref[t * held + rows:(t + 1) * held, :rows][2 * t:2 * t + 2, :])
            for t in range(groups)
        ]
        pick = one_hot(size, 0, jnp.concatenate(ids, axis=1))
        messages = [ref[t * held:t * held + rows, :] for t in range(groups)]
        totals = totals + dot(pick, jnp.concatenate(messages, axis=0))
        counts = counts + count_of(pick)
    new = refresh(totals, counts, state_ref[...], w_ref[...])
    new_ref[...] = new
    reply_ref[...] = dot_t(pick, new).astype(BF)


def update_cust(groups, own, peer, state, weight, after):
    rows = own.shape[0] - groups * id_rows(groups)
    return pl.pallas_call(
        functools.partial(cust_kernel, groups),
        in_specs=[VMEM] * 4 + [ANY] * len(after),
        out_specs=[VMEM] * 2,
        out_shape=[
            jax.ShapeDtypeStruct(state.shape, BF),
            jax.ShapeDtypeStruct((rows, H), BF),
        ],
        compiler_params=PARAMS,
        name="update_cust",
    )(own, peer, state, weight, *after)


def prod_sum_kernel(slabs, parts, ids_ref, *refs):
    blocks, pieces = refs[:parts], refs[-slabs:]
    size = pieces[0].shape[0] - ID_ROWS
    rows = jnp.concatenate([ref[:ref.shape[0] - ID_ROWS, :] for ref in blocks], axis=0)
    ones = jnp.ones((ID_ROWS, rows.shape[0]), BF)
    row = iota((ID_ROWS, size), 0)
    for t, ref in enumerate(pieces):
        owner = lax.axis_index("rev") ^ t
        pick = one_hot(size, owner * size, ids_ref[...])
        counts = dot_nt(ones, pick).astype(jnp.int32)
        halves = jnp.where(row == 0, counts >> 5, jnp.where(row == 1, counts & 31, 0))
        ref[:size, :] = dot(pick, rows).astype(ref.dtype)
        ref[size:, :] = jnp.zeros((ID_ROWS, H), ref.dtype)
        ref[size:, :size] = halves.astype(F32).astype(ref.dtype)


def sum_prod(ids, blocks, size, slabs, after):
    piece = lambda kind: jax.ShapeDtypeStruct((size // slabs + ID_ROWS, H), kind)
    return pl.pallas_call(
        functools.partial(prod_sum_kernel, slabs, len(blocks)),
        in_specs=[VMEM] * (1 + len(blocks)) + [ANY] * len(after),
        out_specs=[VMEM] * slabs,
        out_shape=[piece(F32)] + [piece(BF)] * (slabs - 1),
        compiler_params=PARAMS,
        name="sum_prod",
    )(ids, *blocks, *after)


def prod_update_kernel(slabs, state_ref, w_ref, *rest):
    new_ref = rest[-1]
    size = new_ref.shape[0]
    first = pl.multiple_of(lax.axis_index("rev") * size, size)
    totals = sum(ref[:size, :].astype(F32) for ref in rest[:slabs])
    halves = sum(ref[size:, :size].astype(F32) for ref in rest[:slabs])
    count_row = halves[0:1, :] * 32.0 + halves[1:2, :]
    diagonal = iota((size, size), 0) == iota((size, size), 1)
    counts = jnp.sum(jnp.where(diagonal, count_row, 0.0), axis=1, keepdims=True)
    new_ref[...] = refresh(totals, counts, state_ref[pl.ds(first, size), :], w_ref[...])


def update_prod(state, weight, pieces, after):
    slabs = len(pieces)
    return pl.pallas_call(
        functools.partial(prod_update_kernel, slabs),
        in_specs=[VMEM] * (2 + slabs) + [ANY] * len(after),
        out_specs=VMEM,
        out_shape=jax.ShapeDtypeStruct((state.shape[0] // slabs, H), BF),
        compiler_params=PARAMS,
        name="update_prod",
    )(state, weight, *pieces, *after)


def prod_reply_kernel(slabs, parts, pick_ref, *rest):
    pieces, new_ref, reply_refs = rest[:slabs], rest[-1], rest[-1 - parts:-1]
    size = pieces[0].shape[0]
    for t, ref in enumerate(pieces):
        first = pl.multiple_of((lax.axis_index("rev") ^ t) * size, size)
        new_ref[pl.ds(first, size), :] = ref[...]
    rows = reply_refs[0].shape[0]
    for s, ref in enumerate(reply_refs):
        ref[...] = dot(pick_ref[s * rows:(s + 1) * rows, :], new_ref[...]).astype(BF)


def reply_prod(pick, pieces, parts, after):
    slabs = len(pieces)
    rows = pick.shape[0]
    return pl.pallas_call(
        functools.partial(prod_reply_kernel, slabs, parts),
        in_specs=[VMEM] * (1 + slabs) + [ANY] * len(after),
        out_specs=[VMEM] * parts,
        out_shape=[jax.ShapeDtypeStruct((rows // parts, H), BF)] * parts,
        scratch_shapes=[pltpu.VMEM((pieces[0].shape[0] * slabs, H), BF)],
        compiler_params=PARAMS,
        name="reply_prod",
    )(pick, *pieces, *after)


def states_kernel(cust_ref, *refs):
    pieces, (cust_out, prod_out) = refs[:-2], refs[-2:]
    size = pieces[0].shape[0]
    cust_out[...] = cust_ref[...]
    for t, ref in enumerate(pieces):
        first = pl.multiple_of((lax.axis_index("rev") ^ t) * size, size)
        prod_out[pl.ds(first, size), :] = ref[...]


def states(new_cust, pieces):
    rows = pieces[0].shape[0] * len(pieces)
    return pl.pallas_call(
        states_kernel,
        in_specs=[VMEM] * (1 + len(pieces)),
        out_specs=[VMEM] * 2,
        out_shape=[jax.ShapeDtypeStruct(new_cust.shape, BF), jax.ShapeDtypeStruct((rows, H), BF)],
        compiler_params=PARAMS,
        name="states",
    )(new_cust, *pieces)


def turned_kernel(ids_ref, *refs):
    for n, ref in enumerate(refs):
        rows = iota((ref.shape[1], ref.shape[0]), 0)
        ref[...] = jnp.where(rows == ids_ref[n:n + 1, :], 1.0, 0.0).T.astype(BF)


def turned_picks(ids, size):
    pick = jax.ShapeDtypeStruct((ids.shape[1], size), BF)
    return pl.pallas_call(
        turned_kernel,
        in_specs=[VMEM],
        out_specs=[VMEM] * ids.shape[0],
        out_shape=[pick] * ids.shape[0],
        compiler_params=PARAMS,
        name="turned_picks",
    )(ids)


def finish_part_kernel(start, pick_ref, sum_ref, w_ref, *rest):
    rows = jnp.concatenate([ref[...] for ref in rest[:-1]], axis=0)
    at, wide = start
    back = dot(pick_ref[:, at:at + rows.shape[0]], rows).astype(BF)
    total = sum_ref[...].astype(F32) + dot(back, w_ref[wide:wide + H, :])
    if rest[-1].dtype == BF:
        total = rms_norm(total)
    rest[-1][...] = total.astype(rest[-1].dtype)


def finish_part(start, picks, total, w_back, rows, kind, name):
    return pl.pallas_call(
        functools.partial(finish_part_kernel, start),
        in_specs=[VMEM] * (3 + len(rows)),
        out_specs=VMEM,
        out_shape=jax.ShapeDtypeStruct(total.shape, kind),
        compiler_params=PARAMS,
        name=name,
    )(picks, total, w_back, *rows)


def halve_kernel(parts, *refs):
    half = refs[0].shape[0] // 2
    for u, ref in enumerate(refs[-2:]):
        for s in range(parts):
            ref[s * half:(s + 1) * half, :] = refs[s][u * half:(u + 1) * half, :]


def halve(parts, after):
    rows = sum(part.shape[0] for part in parts) // 2
    return pl.pallas_call(
        functools.partial(halve_kernel, len(parts)),
        in_specs=[VMEM] * len(parts) + [ANY] * len(after),
        out_specs=[VMEM] * 2,
        out_shape=[jax.ShapeDtypeStruct((rows, H), BF)] * 2,
        compiler_params=PARAMS,
        name="halve_product_replies",
    )(*parts, *after)


def swap(value, axis, by):
    if by == 0:
        return value
    return lax.ppermute(value, axis, [(i, i ^ by) for i in range(lax.axis_size(axis))])


def rows_of(parts, start, size):
    return jnp.concatenate([part[start:start + size] for part in parts], axis=0)


def on_device(
    review_cols,
    cust_state,
    prod_state,
    w_qkv,
    w_out,
    w_msg,
    w_cust_up,
    w_prod_up,
    w_back,
    cust_slot,
    prod_slot,
    prod_pos,
    live_count,
):
    rows = review_cols.shape[0]
    nr, nz, nc = lax.axis_size("rev"), lax.axis_size("cust"), lax.axis_size("prod")
    cs = rows // (nr * nz)
    ps = rows // (nz * nc)
    wide = rows // nz
    index = jnp.concatenate(
        [
            prod_pos,
            cust_slot.reshape(1, rows),
            prod_slot.reshape(1, rows),
            jnp.pad(live_count, ((0, 0), (0, rows - nr * nz))),
        ],
        axis=0,
    )
    review_h, order, cust_blocks, prod_blocks = encode(
        (nr, nz, nc), review_cols, w_qkv, w_out, w_msg, index
    )

    cust_pick, prod_pick = turned_picks(order, rows)

    prod_peer = swap(prod_blocks[1], "prod", 1)
    got = [swap(cust_blocks[s], "cust", s) for s in range(nz)]
    prod_blocks = pair(nz, prod_blocks[0], prod_peer, got[1:3])
    prod_got = [swap(prod_blocks[s], "cust", s) for s in range(nz)]

    groups = regroup(cs, nr, got, prod_blocks[1:])
    groups = [swap(groups[t], "rev", t) for t in range(nr)]
    own = join(groups, prod_got[1:3])
    peer = swap(own, "prod", 1)

    prod_in = jnp.concatenate([ids_in(block[wide:, :wide]) for block in prod_got], axis=1)
    pieces = sum_prod(prod_in, prod_got, prod_state.shape[0], nr, [])
    new_cust, reply = update_cust(nr, own, peer, cust_state, w_cust_up, [])
    pieces = [swap(pieces[t], "rev", t) for t in range(nr)]
    blocks = reply.reshape(nr, nz, cs, H)
    cust_got = [swap(blocks[:, s].reshape(wide, H), "cust", s) for s in range(nz)]

    new_piece = update_prod(prod_state, w_prod_up, pieces, cust_got[1:2])
    new_pieces = [swap(new_piece, "rev", t) for t in range(nr)]
    made = reply_prod(turned_picks(prod_in, prod_state.shape[0])[0], new_pieces, nz, cust_got[2:])
    new_cust, new_prod = states(new_cust, new_pieces)
    replies = [swap(made[s], "cust", s) for s in range(nz)]
    cust_back = regroup(cs, nr, cust_got, made[:1])
    cust_back = [swap(cust_back[t], "rev", t) for t in range(nr)]
    part = finish_part((0, 0), cust_pick, review_h, w_back, cust_back, F32, "finish_cust")
    own_replies, peer_replies = halve(replies, [part, new_prod])
    peer_replies = swap(peer_replies, "prod", 1)
    part = finish_part((0, H), prod_pick, part, w_back, [own_replies], F32, "finish_own")
    review_out = finish_part((rows // nc, H), prod_pick, part, w_back, [peer_replies], BF, "finish")
    return (review_out, new_cust, new_prod)


def solution(mesh):
    every = P(("rev", "cust", "prod"))
    in_specs = (
        P(("rev", "cust", "prod"), None),
        P(("rev", "cust"), None),
        P(("cust", "prod"), None),
        P(),
        P(),
        P(),
        P(),
        P(),
        P(),
        every,
        every,
        P(("rev", "cust", "prod"), None),
        P(("rev", "cust", "prod"), None),
    )
    out_specs = (
        P(("rev", "cust", "prod"), None),
        P(("rev", "cust"), None),
        P(("cust", "prod"), None),
    )
    return jax.shard_map(
        on_device, mesh=mesh, in_specs=in_specs, out_specs=out_specs, check_vma=False
    )
```

```python
import functools
import math

import jax
import jax.numpy as jnp
from jax import lax
from jax.experimental import pallas as pl
from jax.experimental.pallas import tpu as pltpu
from jax.sharding import PartitionSpec as P

H = 512
HEADS = 8
NCOL = 4
HD = 64
EPS = 1e-06
BF = jnp.bfloat16
F32 = jnp.float32
ID_ROWS = 16
LANES = 128
VMEM = pl.BlockSpec(memory_space=pltpu.VMEM)
HBM = pl.BlockSpec(memory_space=pltpu.HBM)
ANY = pl.BlockSpec(memory_space=pl.ANY)
PARAMS = pltpu.CompilerParams(vmem_limit_bytes=16 * 1024 * 1024)
ENCODE_PARAMS = pltpu.CompilerParams(vmem_limit_bytes=52 * 1024 * 1024)


def rms_norm(vector):
    return vector * lax.rsqrt(jnp.mean(vector * vector, axis=-1, keepdims=True) + EPS)


def dot(left, right):
    return jnp.dot(left, right, preferred_element_type=F32)


def dot_t(left, right):
    return lax.dot_general(left, right, (((0,), (0,)), ((), ())), preferred_element_type=F32)


def dot_nt(left, right):
    return lax.dot_general(left, right, (((1,), (1,)), ((), ())), preferred_element_type=F32)


def one_hot(rows, first, ids):
    row = lax.broadcasted_iota(jnp.int32, (rows, ids.shape[1]), 0) + first
    return jnp.where(row == ids, 1.0, 0.0).astype(BF)


def iota(shape, dim):
    return lax.broadcasted_iota(jnp.int32, shape, dim)


def encode_rows(tokens, w_qkv, w_out, pair_sum, spread, before):
    rows = tokens[0].shape[0]
    stacked = jnp.concatenate(tokens, axis=0)
    part = []
    for which in range(3):
        before(which)
        made = dot(stacked, w_qkv[:, which * H:(which + 1) * H]).astype(BF)
        part.append([made[c * rows:(c + 1) * rows] for c in range(NCOL)])
    query, key, value = part
    lane = iota((rows, 128), 1)
    scores = jnp.zeros((rows, 128), F32)
    for j in range(NCOL):
        both = dot(jnp.concatenate([query[i] * key[j] for i in range(NCOL)], axis=0), pair_sum)
        for i in range(NCOL):
            scores = jnp.where(lane >> 3 == j * NCOL + i, both[i * rows:(i + 1) * rows], scores)
    scores = scores * (1.0 / math.sqrt(HD))
    top = jnp.maximum(scores, pltpu.roll(scores, 64, 1))
    top = jnp.maximum(top, pltpu.roll(top, 32, 1))
    expon = jnp.exp(scores - top)
    total = expon + pltpu.roll(expon, 64, 1)
    total = total + pltpu.roll(total, 32, 1)
    weight = (expon / total).astype(BF).astype(F32)
    attended = jnp.zeros((rows, H), F32)
    pooled = jnp.zeros((rows, H), F32)
    for j in range(NCOL):
        turned = pltpu.roll(weight, (128 - NCOL * HEADS * j) % 128, 1).astype(BF)
        attended = attended + dot(turned, spread) * value[j].astype(F32)
        pooled = pooled + tokens[j].astype(F32)
    before(3)
    mixed = dot((attended * (1.0 / NCOL)).astype(BF), w_out[...])
    return rms_norm(pooled * (1.0 / NCOL) + mixed).astype(BF)


def halves_at(ids, place, count):
    row = iota((count, ids.shape[1]), 0)
    halves = jnp.where((row & 1) == 0, ids >> 5, ids & 31)
    return jnp.where(row >> 1 == place, halves, 0).astype(F32).astype(BF)


def id_rows(count):
    return -(-2 * count // ID_ROWS) * ID_ROWS


def split(index, size):
    if size & (size - 1) == 0:
        return index >> (size.bit_length() - 1), index & (size - 1)
    return lax.div(index, size), lax.rem(index, size)


def send_orders(sizes, index_ref):
    nr, nz, nc = sizes
    rows = index_ref.shape[1]
    cs, ps = rows // (nr * nz), rows // (nz * nc)
    mr, mz, mc = lax.axis_index("rev"), lax.axis_index("cust"), lax.axis_index("prod")
    pos, cust_slot, prod_slot = (index_ref[n:n + 1, :] for n in range(3))
    block, k = split(iota((1, rows), 1), cs)
    r, z = split(block, nz)
    counts = index_ref[3:4, :LANES].astype(F32).astype(BF)
    live = dot(counts, one_hot(LANES, 0, block)).astype(jnp.int32)
    cust = mz ^ z, mr ^ r, k, jnp.where(k < live, cust_slot + 1, 0)
    prod_id = jnp.where(k < live, prod_slot + 1, 0)
    block, k = split(pos, ps)
    z, c = split(block, nc)
    return cust, (mz ^ z, mc ^ c, k, prod_id)


def encode_kernel(sizes, rows, *refs):
    x_hbm, w_qkv_hbm, w_out_hbm, w_msg_hbm, index_ref, h_ref, order_ref = refs[:7]
    x_ref, w_qkv, w_out, w_msg, cust_rows, sem = refs[-6:]
    nr, nz, nc = sizes
    cust_refs, prod_refs = refs[7:7 + nz], refs[7 + nz:-6]
    chunks = x_hbm.shape[0] // rows
    copy = pltpu.make_async_copy
    x_copies = [
        copy(x_hbm.at[pl.ds(c * rows, rows)], x_ref.at[pl.ds(c * rows, rows)], sem.at[c])
        for c in range(chunks)
    ]
    w_copies = [
        copy(w_qkv_hbm.at[:, pl.ds(k * H, H)], w_qkv.at[:, pl.ds(k * H, H)], sem.at[chunks + k])
        for k in range(3)
    ]
    w_copies.append(copy(w_out_hbm, w_out, sem.at[chunks + 3]))
    last = copy(w_msg_hbm, w_msg, sem.at[chunks + 4])
    x_copies[0].start()
    w_copies[0].start()
    w_copies[1].start()
    pair_sum = jnp.where(iota((H, 128), 0) >> 6 == (iota((H, 128), 1) & 7), 1.0, 0.0).astype(BF)
    spread = jnp.where(
        (iota((128, H), 0) < NCOL * HEADS) & ((iota((128, H), 0) & 7) == iota((128, H), 1) >> 6),
        1.0,
        0.0,
    ).astype(BF)

    def first_before(which):
        w_copies[which].wait()
        if which == 0:
            w_copies[2].start()
            for x_copy in x_copies[1:]:
                x_copy.start()
        if which == 1:
            w_copies[3].start()
            last.start()

    for c in range(chunks):
        x_copies[c].wait()
        at = slice(c * rows, (c + 1) * rows)
        tokens = [x_ref[at, k * H:(k + 1) * H] for k in range(NCOL)]
        before = first_before if c == 0 else lambda which: None
        h_ref[at, :] = encode_rows(tokens, w_qkv, w_out, pair_sum, spread, before)
    (s_of, t_of, k, ids), (ps_of, u_of, pk, prod_ids) = send_orders(sizes, index_ref)
    count = h_ref.shape[0]
    cs, ps = count // (nr * nz), count // (nz * nc)
    cust_sent, prod_sent = (s_of * nr + t_of) * cs + k, (u_of * nz + ps_of) * ps + pk
    order_ref[0:1, :] = (t_of * nz + s_of) * cs + k
    order_ref[1:2, :] = prod_sent
    lanes = one_hot(nz * cs, 0, s_of * cs + k)
    halves = halves_at(ids, t_of, id_rows(nr))
    cust_ids = [
        dot_nt(jnp.where(s_of == s, halves, jnp.zeros_like(halves)), lanes) for s in range(nz)
    ]
    lanes = one_hot(nc * ps, 0, u_of * ps + pk)
    halves = halves_at(prod_ids, ps_of * (ID_ROWS // 2), nz * ID_ROWS)
    prod_ids = [
        dot_nt(jnp.where(u_of == u, halves, jnp.zeros_like(halves)), lanes) for u in range(nc)
    ]
    last.wait()
    message = dot(h_ref[...], w_msg[...]).astype(BF)
    cust_rows[...] = message[:, :H]
    for sent, made, refs, which in (
        (cust_sent, cust_ids, cust_refs, 0),
        (prod_sent, prod_ids, prod_refs, 1),
    ):
        size = count // len(refs)
        for s, ref in enumerate(refs):
            if which == 0 and cs % 16 == 0:
                z = lax.axis_index("cust") ^ s
                for t in range(nr):
                    first = pl.multiple_of(((lax.axis_index("rev") ^ t) * nz + z) * cs, cs)
                    ref[t * cs:(t + 1) * cs, :] = cust_rows[pl.ds(first, cs), :]
            else:
                pick = one_hot(size, s * size, sent)
                ref[:size, :] = dot(pick, message[:, which * H:(which + 1) * H]).astype(BF)
            ref[size:, :] = jnp.zeros((ref.shape[0] - size, H), BF)
            ref[size:, :made[s].shape[1]] = made[s].astype(BF)


def encode(sizes, review_cols, w_qkv, w_out, w_msg, index):
    count = review_cols.shape[0]
    nr, nz, nc = sizes
    rows = min(count, 256)
    cust_block = jax.ShapeDtypeStruct((count // nz + id_rows(nr), H), BF)
    prod_block = jax.ShapeDtypeStruct((count // nc + nz * ID_ROWS, H), BF)
    out = pl.pallas_call(
        functools.partial(encode_kernel, sizes, rows),
        in_specs=[HBM] * 4 + [VMEM],
        out_specs=[VMEM] * (2 + nz + nc),
        out_shape=[
            jax.ShapeDtypeStruct((count, H), BF),
            jax.ShapeDtypeStruct((2, count), jnp.int32),
        ]
        + [cust_block] * nz
        + [prod_block] * nc,
        scratch_shapes=[pltpu.VMEM(a.shape, BF) for a in (review_cols, w_qkv, w_out, w_msg)]
        + [pltpu.VMEM((count, H), BF)]
        + [pltpu.SemaphoreType.DMA((count // rows + 5,))],
        compiler_params=ENCODE_PARAMS,
        name="encode",
    )(review_cols, w_qkv, w_out, w_msg, index)
    return out[0], out[1], out[2:2 + nz], out[2 + nz:]


def pair_kernel(parts, own_ref, peer_ref, *refs):
    part = (own_ref.shape[0] - parts * ID_ROWS) // parts
    for s, ref in enumerate(refs[-parts:]):
        at = parts * part + s * ID_ROWS
        ref[:part, :] = own_ref[s * part:(s + 1) * part, :]
        ref[part:2 * part, :] = peer_ref[s * part:(s + 1) * part, :]
        ref[2 * part:, :] = own_ref[at:at + ID_ROWS, :] + peer_ref[at:at + ID_ROWS, :]


def pair(parts, own, peer, after):
    part = (own.shape[0] - parts * ID_ROWS) // parts
    return pl.pallas_call(
        functools.partial(pair_kernel, parts),
        in_specs=[VMEM] * 2 + [ANY] * len(after),
        out_specs=[VMEM] * parts,
        out_shape=[jax.ShapeDtypeStruct((2 * part + ID_ROWS, H), BF)] * parts,
        compiler_params=PARAMS,
        name="pair_product_blocks",
    )(own, peer, *after)


def regroup_kernel(size, parts, groups, *refs):
    held = groups * size
    for t, ref in enumerate(refs[-groups:]):
        for s in range(parts):
            ref[s * size:(s + 1) * size, :] = refs[s][t * size:(t + 1) * size, :]
        if held < refs[0].shape[0]:
            ref[parts * size:, :] = sum(refs[s][held:, :] for s in range(parts))


def regroup(size, groups, got, after):
    parts, ids = len(got), got[0].shape[0] - groups * size
    if size % 16:
        tail = sum(p[groups * size:] for p in got)
        return [
            jnp.concatenate([p[t * size:(t + 1) * size] for p in got] + [tail], axis=0)
            for t in range(groups)
        ]
    return pl.pallas_call(
        functools.partial(regroup_kernel, size, parts, groups),
        in_specs=[VMEM] * parts + [ANY] * len(after),
        out_specs=[VMEM] * groups,
        out_shape=[jax.ShapeDtypeStruct((parts * size + ids, H), BF)] * groups,
        compiler_params=PARAMS,
        name="regroup_customer_blocks",
    )(*got, *after)


def join_kernel(count, *refs):
    at = 0
    for ref in refs[:count]:
        refs[-1][at:at + ref.shape[0], :] = ref[...]
        at += ref.shape[0]


def join(parts, after):
    rows = sum(part.shape[0] for part in parts)
    return pl.pallas_call(
        functools.partial(join_kernel, len(parts)),
        in_specs=[VMEM] * len(parts) + [ANY] * len(after),
        out_specs=VMEM,
        out_shape=jax.ShapeDtypeStruct((rows, H), BF),
        compiler_params=PARAMS,
        name="join",
    )(*parts, *after)


def refresh(totals, counts, states, weight):
    average = (totals / jnp.sqrt(jnp.maximum(counts, 1.0))).astype(BF)
    update = dot(average, weight)
    update = update * (1.0 / (1.0 + jnp.exp(-update)))
    return rms_norm(states.astype(F32) + update).astype(BF)


def count_of(pick):
    return jnp.sum(pick.astype(F32), axis=1, keepdims=True)


def ids_in(rows):
    rows = rows.astype(F32)
    return (rows[0:1, :] * 32.0 + rows[1:2, :]).astype(jnp.int32) - 1


def cust_kernel(groups, own_ref, peer_ref, state_ref, w_ref, *refs):
    new_ref, reply_ref = refs[-2:]
    size = state_ref.shape[0]
    held = own_ref.shape[0] // groups
    rows = held - id_rows(groups)
    totals, counts = jnp.zeros((size, H), F32), jnp.zeros((size, 1), F32)
    for ref in (peer_ref, own_ref):
        ids = [
            ids_in(ref[t * held + rows:(t + 1) * held, :rows][2 * t:2 * t + 2, :])
            for t in range(groups)
        ]
        pick = one_hot(size, 0, jnp.concatenate(ids, axis=1))
        messages = [ref[t * held:t * held + rows, :] for t in range(groups)]
        totals = totals + dot(pick, jnp.concatenate(messages, axis=0))
        counts = counts + count_of(pick)
    new = refresh(totals, counts, state_ref[...], w_ref[...])
    new_ref[...] = new
    reply_ref[...] = dot_t(pick, new).astype(BF)


def update_cust(groups, own, peer, state, weight, after):
    rows = own.shape[0] - groups * id_rows(groups)
    return pl.pallas_call(
        functools.partial(cust_kernel, groups),
        in_specs=[VMEM] * 4 + [ANY] * len(after),
        out_specs=[VMEM] * 2,
        out_shape=[
            jax.ShapeDtypeStruct(state.shape, BF),
            jax.ShapeDtypeStruct((rows, H), BF),
        ],
        compiler_params=PARAMS,
        name="update_cust",
    )(own, peer, state, weight, *after)


def prod_sum_kernel(slabs, parts, ids_ref, *refs):
    blocks, pieces = refs[:parts], refs[-slabs:]
    size = pieces[0].shape[0] - ID_ROWS
    rows = jnp.concatenate([ref[:ref.shape[0] - ID_ROWS, :] for ref in blocks], axis=0)
    ones = jnp.ones((ID_ROWS, rows.shape[0]), BF)
    row = iota((ID_ROWS, size), 0)
    for t, ref in enumerate(pieces):
        owner = lax.axis_index("rev") ^ t
        pick = one_hot(size, owner * size, ids_ref[...])
        counts = dot_nt(ones, pick).astype(jnp.int32)
        halves = jnp.where(row == 0, counts >> 5, jnp.where(row == 1, counts & 31, 0))
        ref[:size, :] = dot(pick, rows).astype(ref.dtype)
        ref[size:, :] = jnp.zeros((ID_ROWS, H), ref.dtype)
        ref[size:, :size] = halves.astype(F32).astype(ref.dtype)


def sum_prod(ids, blocks, size, slabs, after):
    piece = lambda kind: jax.ShapeDtypeStruct((size // slabs + ID_ROWS, H), kind)
    return pl.pallas_call(
        functools.partial(prod_sum_kernel, slabs, len(blocks)),
        in_specs=[VMEM] * (1 + len(blocks)) + [ANY] * len(after),
        out_specs=[VMEM] * slabs,
        out_shape=[piece(F32)] + [piece(BF)] * (slabs - 1),
        compiler_params=PARAMS,
        name="sum_prod",
    )(ids, *blocks, *after)


def prod_update_kernel(slabs, state_ref, w_ref, *rest):
    new_ref = rest[-1]
    size = new_ref.shape[0]
    first = pl.multiple_of(lax.axis_index("rev") * size, size)
    totals = sum(ref[:size, :].astype(F32) for ref in rest[:slabs])
    halves = sum(ref[size:, :size].astype(F32) for ref in rest[:slabs])
    count_row = halves[0:1, :] * 32.0 + halves[1:2, :]
    diagonal = iota((size, size), 0) == iota((size, size), 1)
    counts = jnp.sum(jnp.where(diagonal, count_row, 0.0), axis=1, keepdims=True)
    new_ref[...] = refresh(totals, counts, state_ref[pl.ds(first, size), :], w_ref[...])


def update_prod(state, weight, pieces, after):
    slabs = len(pieces)
    return pl.pallas_call(
        functools.partial(prod_update_kernel, slabs),
        in_specs=[VMEM] * (2 + slabs) + [ANY] * len(after),
        out_specs=VMEM,
        out_shape=jax.ShapeDtypeStruct((state.shape[0] // slabs, H), BF),
        compiler_params=PARAMS,
        name="update_prod",
    )(state, weight, *pieces, *after)


def prod_reply_kernel(slabs, parts, pick_ref, *rest):
    pieces, new_ref, reply_refs = rest[:slabs], rest[-1], rest[-1 - parts:-1]
    size = pieces[0].shape[0]
    for t, ref in enumerate(pieces):
        first = pl.multiple_of((lax.axis_index("rev") ^ t) * size, size)
        new_ref[pl.ds(first, size), :] = ref[...]
    rows = reply_refs[0].shape[0]
    for s, ref in enumerate(reply_refs):
        ref[...] = dot(pick_ref[s * rows:(s + 1) * rows, :], new_ref[...]).astype(BF)


def reply_prod(pick, pieces, parts, after):
    slabs = len(pieces)
    rows = pick.shape[0]
    return pl.pallas_call(
        functools.partial(prod_reply_kernel, slabs, parts),
        in_specs=[VMEM] * (1 + slabs) + [ANY] * len(after),
        out_specs=[VMEM] * parts,
        out_shape=[jax.ShapeDtypeStruct((rows // parts, H), BF)] * parts,
        scratch_shapes=[pltpu.VMEM((pieces[0].shape[0] * slabs, H), BF)],
        compiler_params=PARAMS,
        name="reply_prod",
    )(pick, *pieces, *after)


def states_kernel(cust_ref, *refs):
    pieces, (cust_out, prod_out) = refs[:-2], refs[-2:]
    size = pieces[0].shape[0]
    cust_out[...] = cust_ref[...]
    for t, ref in enumerate(pieces):
        first = pl.multiple_of((lax.axis_index("rev") ^ t) * size, size)
        prod_out[pl.ds(first, size), :] = ref[...]


def states(new_cust, pieces):
    rows = pieces[0].shape[0] * len(pieces)
    return pl.pallas_call(
        states_kernel,
        in_specs=[VMEM] * (1 + len(pieces)),
        out_specs=[VMEM] * 2,
        out_shape=[jax.ShapeDtypeStruct(new_cust.shape, BF), jax.ShapeDtypeStruct((rows, H), BF)],
        compiler_params=PARAMS,
        name="states",
    )(new_cust, *pieces)


def turned_kernel(ids_ref, *refs):
    for n, ref in enumerate(refs):
        rows = iota((ref.shape[1], ref.shape[0]), 0)
        ref[...] = jnp.where(rows == ids_ref[n:n + 1, :], 1.0, 0.0).T.astype(BF)


def turned_picks(ids, size):
    pick = jax.ShapeDtypeStruct((ids.shape[1], size), BF)
    return pl.pallas_call(
        turned_kernel,
        in_specs=[VMEM],
        out_specs=[VMEM] * ids.shape[0],
        out_shape=[pick] * ids.shape[0],
        compiler_params=PARAMS,
        name="turned_picks",
    )(ids)


def finish_part_kernel(start, pick_ref, sum_ref, w_ref, *rest):
    rows = jnp.concatenate([ref[...] for ref in rest[:-1]], axis=0)
    at, wide = start
    back = dot(pick_ref[:, at:at + rows.shape[0]], rows).astype(BF)
    total = sum_ref[...].astype(F32) + dot(back, w_ref[wide:wide + H, :])
    if rest[-1].dtype == BF:
        total = rms_norm(total)
    rest[-1][...] = total.astype(rest[-1].dtype)


def finish_part(start, picks, total, w_back, rows, kind, name):
    return pl.pallas_call(
        functools.partial(finish_part_kernel, start),
        in_specs=[VMEM] * (3 + len(rows)),
        out_specs=VMEM,
        out_shape=jax.ShapeDtypeStruct(total.shape, kind),
        compiler_params=PARAMS,
        name=name,
    )(picks, total, w_back, *rows)


def halve_kernel(parts, *refs):
    half = refs[0].shape[0] // 2
    for u, ref in enumerate(refs[-2:]):
        for s in range(parts):
            ref[s * half:(s + 1) * half, :] = refs[s][u * half:(u + 1) * half, :]


def halve(parts, after):
    rows = sum(part.shape[0] for part in parts) // 2
    return pl.pallas_call(
        functools.partial(halve_kernel, len(parts)),
        in_specs=[VMEM] * len(parts) + [ANY] * len(after),
        out_specs=[VMEM] * 2,
        out_shape=[jax.ShapeDtypeStruct((rows, H), BF)] * 2,
        compiler_params=PARAMS,
        name="halve_product_replies",
    )(*parts, *after)


def swap(value, axis, by):
    if by == 0:
        return value
    return lax.ppermute(value, axis, [(i, i ^ by) for i in range(lax.axis_size(axis))])


def rows_of(parts, start, size):
    return jnp.concatenate([part[start:start + size] for part in parts], axis=0)


def on_device(
    review_cols,
    cust_state,
    prod_state,
    w_qkv,
    w_out,
    w_msg,
    w_cust_up,
    w_prod_up,
    w_back,
    cust_slot,
    prod_slot,
    prod_pos,
    live_count,
):
    rows = review_cols.shape[0]
    nr, nz, nc = lax.axis_size("rev"), lax.axis_size("cust"), lax.axis_size("prod")
    cs = rows // (nr * nz)
    ps = rows // (nz * nc)
    wide = rows // nz
    index = jnp.concatenate(
        [
            prod_pos,
            cust_slot.reshape(1, rows),
            prod_slot.reshape(1, rows),
            jnp.pad(live_count, ((0, 0), (0, rows - nr * nz))),
        ],
        axis=0,
    )
    review_h, order, cust_blocks, prod_blocks = encode(
        (nr, nz, nc), review_cols, w_qkv, w_out, w_msg, index
    )

    cust_pick, prod_pick = turned_picks(order, rows)

    prod_peer = swap(prod_blocks[1], "prod", 1)
    got = [swap(cust_blocks[s], "cust", s) for s in range(nz)]
    prod_blocks = pair(nz, prod_blocks[0], prod_peer, got[1:3])
    prod_got = [swap(prod_blocks[s], "cust", s) for s in range(nz)]

    groups = regroup(cs, nr, got, prod_blocks[1:])
    groups = [swap(groups[t], "rev", t) for t in range(nr)]
    own = join(groups, prod_got[1:3])
    peer = swap(own, "prod", 1)

    prod_in = jnp.concatenate([ids_in(block[wide:, :wide]) for block in prod_got], axis=1)
    pieces = sum_prod(prod_in, prod_got, prod_state.shape[0], nr, [])
    new_cust, reply = update_cust(nr, own, peer, cust_state, w_cust_up, [])
    pieces = [swap(pieces[t], "rev", t) for t in range(nr)]
    blocks = reply.reshape(nr, nz, cs, H)
    cust_got = [swap(blocks[:, s].reshape(wide, H), "cust", s) for s in range(nz)]

    new_piece = update_prod(prod_state, w_prod_up, pieces, cust_got[1:2])
    new_pieces = [swap(new_piece, "rev", t) for t in range(nr)]
    made = reply_prod(turned_picks(prod_in, prod_state.shape[0])[0], new_pieces, nz, cust_got[2:])
    new_cust, new_prod = states(new_cust, new_pieces)
    replies = [swap(made[s], "cust", s) for s in range(nz)]
    cust_back = regroup(cs, nr, cust_got, made[:1])
    cust_back = [swap(cust_back[t], "rev", t) for t in range(nr)]
    part = finish_part((0, 0), cust_pick, review_h, w_back, cust_back, F32, "finish_cust")
    early, late = halve(replies[:nz // 2], []), halve(replies[nz // 2:], [part, new_prod])
    peers = [swap(early[1], "prod", 1), swap(late[1], "prod", 1)]
    part = finish_part((0, H), prod_pick, part, w_back, [early[0], late[0]], F32, "finish_own")
    review_out = finish_part((rows // nc, H), prod_pick, part, w_back, peers, BF, "finish")
    return (review_out, new_cust, new_prod)


def solution(mesh):
    every = P(("rev", "cust", "prod"))
    in_specs = (
        P(("rev", "cust", "prod"), None),
        P(("rev", "cust"), None),
        P(("cust", "prod"), None),
        P(),
        P(),
        P(),
        P(),
        P(),
        P(),
        every,
        every,
        P(("rev", "cust", "prod"), None),
        P(("rev", "cust", "prod"), None),
    )
    out_specs = (
        P(("rev", "cust", "prod"), None),
        P(("rev", "cust"), None),
        P(("cust", "prod"), None),
    )
    return jax.shard_map(
        on_device, mesh=mesh, in_specs=in_specs, out_specs=out_specs, check_vma=False
    )
```
